512 devices in a mesh: patch: 64 (over z, y_hi, x), head: 8 (over y_lo, core).
Axes of the slice: x: 4, y: 8 (y_hi: 2, y_lo: 4; y = y_hi * 4 + y_lo), z: 8, core: 2. Of those that a mesh axis runs over, the one named last changes fastest.
Arguments:
- inputs: bfloat16 [2, 2048, 3072], P(None, 'patch', 'head'), may hold values from -111 to 111
- stale_kv: bfloat16 [2, 2048, 2048], P(None, 'patch', 'head'), may hold values from -16 to 16
- w_qkv: bfloat16 [3072, 3, 2048], P(None, None, 'head'), may hold values from -4 to 4
- w_out: bfloat16 [2048, 3072], P('head', 'patch'), may hold values from -0.375 to 0.375
- mod_table: float32 [4, 3, 3072], P(None, None, 'head'), may hold values from -2 to 2
- step_ids: int32 [2], replicated, may hold values from 0 to 3
- slab_order: int32 [64], P('patch'), may hold values from 0 to 63, each once
Outputs:
- branch: bfloat16 [2, 2048, 3072], P(None, 'patch', 'head')
The draws below stay inside these ranges and needn't reach their ends.
Inputs may be any that keep to these rules, and one draw needn't show every extreme that they name: `slab_order`: every slab number once.
All inputs are finite; a program needn't handle non-finite values.
Results may differ from the reference program's by a relative error of at most 0.02.
Values may be sent and summed in bfloat16 or wider, within the bound.
A program may use at most 64 MiB of HBM per device.

```python
import math
import jax
import jax.numpy as jnp
from jax import lax

D = 3072
DH = 128
TOK_DEV = 32
STEPS = 2
TABLE = 4
HEADS = 16
TOKENS = 2048
N_PATCH = 64


def draw_inputs(key, part):
    key = jax.random.fold_in(key, 11)
    key_base = jax.random.fold_in(key, 0)
    col_ramp = 3.0 ** (jnp.arange(D, dtype=jnp.float32) / (D - 1))
    drawn = jnp.clip(jax.random.normal(key_base, (STEPS, TOKENS, D), jnp.float32), -4.0, 4.0) * col_ramp
    return drawn.astype(jnp.bfloat16)


def draw_stale_kv(key, part):
    key = jax.random.fold_in(key, 37)
    key_keys, key_rows, key_vals = jax.random.split(key, 3)
    head_shape = (TOKENS, HEADS, DH)
    row_scale = jnp.exp(jax.random.uniform(key_rows, (TOKENS, HEADS, 1), jnp.float32, math.log(0.08), math.log(0.8)))
    key_part = jnp.clip(jax.random.normal(key_keys, head_shape, jnp.float32), -4.0, 4.0) * row_scale
    value_part = 8.0 * jnp.clip(jax.random.normal(key_vals, head_shape, jnp.float32), -2.0, 2.0)
    drawn = jnp.stack([key_part.reshape(TOKENS, HEADS * DH), value_part.reshape(TOKENS, HEADS * DH)])
    return drawn.astype(jnp.bfloat16)


def draw_w_qkv(key, part):
    key = jax.random.fold_in(key, 53)
    key_base = jax.random.fold_in(key, 0)
    base_vals = jnp.clip(jax.random.normal(key_base, (D, 3, HEADS * DH), jnp.float32), -4.0, 4.0) / D ** 0.5
    slot_gain = jnp.array([1.0, 0.8, 8.0], jnp.float32)[None, :, None]
    gain_all = slot_gain
    return (base_vals * gain_all).astype(jnp.bfloat16)


def draw_mod_table(key, part):
    key = jax.random.fold_in(key, 23)
    key_shift, key_scale, key_gate, key_sign = jax.random.split(key, 4)
    shifting = 0.5 * jnp.clip(jax.random.normal(key_shift, (TABLE, 1, D), jnp.float32), -2.0, 2.0)
    signs = 2.0 * jax.random.randint(key_sign, (TABLE, 1, D), 0, 2).astype(jnp.float32) - 1.0
    scaling = 0.5 * jnp.clip(jax.random.normal(key_scale, (TABLE, 1, D), jnp.float32), -2.0, 2.0)
    gating = signs * jax.random.uniform(key_gate, (TABLE, 1, D), jnp.float32, 0.4, 2.0)
    return jnp.concatenate([shifting, scaling, gating], axis=1)


def strengthened(entries, stream_key, source, target, parts, factor):
    def block_of(dim):
        return (jnp.arange(entries.shape[dim]) // (entries.shape[dim] // parts)).reshape((-1,) + (1,) * (entries.ndim - 1 - dim))

    first = jax.random.permutation(stream_key, parts)[block_of(target)]
    far = (block_of(target) + parts // 2) % parts
    return jnp.where((block_of(source) == first) | (block_of(source) == far), factor * entries, entries)


def levels(key, shape, cuts, low, top_value):
    gain = 1.0
    for position, parts in cuts:
        draws = jax.random.uniform(jax.random.fold_in(jax.random.fold_in(key, 6), position), (parts,), jnp.float32, low / len(cuts), top_value / len(cuts))
        gain = gain * jnp.repeat(jnp.exp(draws), shape[position] // parts).reshape((-1,) + (1,) * (len(shape) - 1 - position))
    return gain


def gaussian_with(stream_key, shape, width, limit, cuts, heavy, kind=jnp.bfloat16):
    entries = width * jax.random.normal(stream_key, shape, jnp.float32)
    if cuts:
        entries = entries * levels(stream_key, shape, cuts, -0.22, 0.18)
    return jnp.clip(strengthened(entries, jax.random.fold_in(stream_key, 3), *heavy), -limit, limit).astype(kind)


def setup_inputs(seed: int = 0) -> dict:
    splits = jax.random.split(jax.random.key(seed), 8)
    inputs = draw_inputs(jax.random.fold_in(splits[7], 71), 0)
    stale_kv = draw_stale_kv(jax.random.fold_in(splits[7], 71), 0)
    w_qkv = draw_w_qkv(jax.random.fold_in(splits[7], 71), 0)
    w_out = gaussian_with(splits[3], (HEADS * DH, D), (HEADS * DH) ** -0.5, 0.375, ((0, 8), (1, 64)), (0, 1, 64, 4.0))
    mod_table = draw_mod_table(jax.random.fold_in(splits[7], 71), 0)
    step_ids = jax.random.randint(splits[5], (STEPS,), 0, TABLE).astype(jnp.int32)
    slab_order = jax.random.permutation(splits[6], N_PATCH).astype(jnp.int32)
    return dict(inputs=inputs, stale_kv=stale_kv, w_qkv=w_qkv, w_out=w_out, mod_table=mod_table, step_ids=step_ids, slab_order=slab_order)


def angle_tables(positions, head_size):
    half_size = head_size // 2
    frequency = 10000.0 ** (-(2.0 * jnp.arange(half_size, dtype=jnp.float32)) / head_size)
    angle_grid = positions.astype(jnp.float32)[:, None] * frequency[None, :]
    return (jnp.cos(angle_grid)[:, None, :], jnp.sin(angle_grid)[:, None, :])

def rotate(values, cos_table, sin_table):
    half_size = values.shape[-1] // 2
    front_half = values[..., :half_size]
    back_half = values[..., half_size:]
    return jnp.concatenate([front_half * cos_table - back_half * sin_table, front_half * sin_table + back_half * cos_table], axis=-1)

def reference(inputs, stale_kv, w_qkv, w_out, mod_table, step_ids, slab_order):
    row_ids = jnp.arange(TOKENS, dtype=jnp.int32)
    positions = slab_order[row_ids // TOK_DEV] * TOK_DEV + row_ids % TOK_DEV
    cos_table, sin_table = angle_tables(positions, DH)
    inv_root = 1.0 / math.sqrt(DH)
    previous_k = stale_kv[0].reshape(TOKENS, HEADS, DH)
    previous_v = stale_kv[1].reshape(TOKENS, HEADS, DH)
    w_flat = w_qkv.reshape(D, 3 * HEADS * DH)
    results = []
    for step in range(STEPS):
        modulation = mod_table[step_ids[step]]
        hidden = inputs[step].astype(jnp.float32)
        row_mean = lax.optimization_barrier(jnp.sum(hidden, axis=1, keepdims=True)) / D
        row_square = lax.optimization_barrier(jnp.sum(hidden * hidden, axis=1, keepdims=True)) / D
        inv_scale = lax.rsqrt(row_square - row_mean * row_mean + 1e-06)
        normed = ((hidden - row_mean) * inv_scale * (1.0 + modulation[1]) + modulation[0]).astype(jnp.bfloat16)
        projected = jnp.dot(normed, w_flat, preferred_element_type=jnp.float32).reshape(TOKENS, 3, HEADS, DH)
        queries = rotate(projected[:, 0], cos_table, sin_table).astype(jnp.bfloat16)
        fresh_k = rotate(projected[:, 1], cos_table, sin_table).astype(jnp.bfloat16)
        fresh_v = projected[:, 2].astype(jnp.bfloat16)

        def attend_slab(slab_rank):
            offset = slab_rank * TOK_DEV
            slab_q = lax.dynamic_slice_in_dim(queries, offset, TOK_DEV, 0)
            key_rows = lax.dynamic_update_slice_in_dim(previous_k, lax.dynamic_slice_in_dim(fresh_k, offset, TOK_DEV, 0), offset, 0)
            value_rows = lax.dynamic_update_slice_in_dim(previous_v, lax.dynamic_slice_in_dim(fresh_v, offset, TOK_DEV, 0), offset, 0)
            scores = jnp.einsum('qhd,khd->hqk', slab_q.astype(jnp.float32), key_rows.astype(jnp.float32)) * inv_root
            row_max = lax.optimization_barrier(jnp.max(scores, axis=2, keepdims=True))
            weights = jnp.exp(scores - row_max)
            totals = lax.optimization_barrier(jnp.sum(weights, axis=2))
            rounded = lax.optimization_barrier(weights.astype(jnp.bfloat16))
            mixed = jnp.einsum('hqk,khd->qhd', rounded.astype(jnp.float32), value_rows.astype(jnp.float32))
            return (mixed / jnp.transpose(totals)[:, :, None]).astype(jnp.bfloat16)
        attended = lax.map(attend_slab, jnp.arange(N_PATCH, dtype=jnp.int32)).reshape(TOKENS, HEADS * DH)
        projected_out = jnp.dot(attended, w_out, preferred_element_type=jnp.float32)
        results.append((modulation[2] * projected_out).astype(jnp.bfloat16))
        previous_k, previous_v = (fresh_k, fresh_v)
    return jnp.stack(results)
```

```python
import functools
import math

import jax
import jax.numpy as jnp
from jax import lax
from jax.experimental import pallas as pl
from jax.experimental.pallas import tpu as pltpu
from jax.sharding import PartitionSpec as P

DH = 128
TOK = 32
FEAT = 384
HC = 256
WIDTH = 3072
OUTC = 48
NZ, NYH, NX, NYL = 8, 2, 4, 4
NB = NYH * NX
F32 = jnp.float32
BF16 = jnp.bfloat16
MESH = pl.DeviceIdType.MESH


def dot_nt(a, b):
    return lax.dot_general(a, b, (((1,), (1,)), ((), ())), preferred_element_type=F32)


def dot_nn(a, b):
    return jnp.dot(a, b, preferred_element_type=F32)


def kernel(
    x_ref, stale_ref, w_ref, wo_ref, mod_ref, ids_ref, cos_ref, sin_ref, out_ref,
    w_v, xg, mg, a_v, kvs, kvf, kv1, qb, os_, orc, wo, e0s, e0r, e1s, e1r, acc,
    w_sem, xs_sem, xr_sem, ms_sem, mr_sem,
    ss_sem, sr_sem, fs_sem, fr_sem, qs_sem, qr_sem, os_sem, or_sem,
    wys_sem, wyr_sem, wzs_sem, wzr_sem, wxs_sem, wxr_sem,
    e0s_sem, e0r_sem, e1s_sem, e1r_sem,
):
    p = lax.axis_index("patch")
    h = lax.axis_index("head")
    z, b = p // NB, p % NB
    yh, x = b // NX, b % NX
    yl, c = h // 2, h % 2

    def z_peer(d):
        return (((z + d) % NZ) * NB + b, h)

    def x_peer(d):
        return (z * NB + yh * NX + (x + d) % NX, h)

    yh_peer = (z * NB + (1 - yh) * NX + x, h)
    sibling = (p, yl * 2 + 1 - c)

    def y_peer(d):
        return (p, ((yl + d) % NYL) * 2 + c)

    peers = [sibling, yh_peer]
    peers += [y_peer(d) for d in range(1, NYL)]
    peers += [x_peer(d) for d in range(1, NX)]
    peers += [z_peer(d) for d in range(1, NZ)]

    barrier = pltpu.get_barrier_semaphore()
    for peer in peers:
        pl.semaphore_signal(barrier, inc=1, device_id=peer, device_id_type=MESH)

    sent = []

    def send(src, dst, ssem, rsem, peer):
        copy = pltpu.make_async_remote_copy(
            src_ref=src, dst_ref=dst, send_sem=ssem, recv_sem=rsem, device_id=peer, device_id_type=MESH
        )
        copy.start()
        sent.append(copy)

    def arrived(dst, ssem, rsem, peer):
        pltpu.make_async_remote_copy(
            src_ref=dst, dst_ref=dst, send_sem=ssem, recv_sem=rsem, device_id=peer, device_id_type=MESH
        ).wait_recv()

    loads = [pltpu.make_async_copy(w_ref.at[t], w_v.at[t], w_sem.at[t]) for t in range(3)]
    for t in (1, 2, 0):
        loads[t].start()

    table_row = lax.broadcasted_iota(jnp.int32, (4, FEAT), 0)
    gates = []
    for s in range(2):
        pick = table_row == ids_ref[s]
        rows = [jnp.sum(jnp.where(pick, mod_ref[k], 0.0), axis=0, keepdims=True) for k in range(3)]
        mg[h, s : s + 1] = rows[0]
        mg[h, 2 + s : 3 + s] = rows[1]
        gates.append(rows[2])
    xg[h] = x_ref[...]
    kvs[0] = stale_ref[...]
    wo[z, yh, x] = wo_ref[...]

    pl.semaphore_wait(barrier, len(peers))

    for d in (2, 1, 3):
        send(xg.at[h], xg.at[h], xs_sem.at[d], xr_sem.at[h], y_peer(d))
        send(mg.at[h], mg.at[h], ms_sem.at[d], mr_sem.at[h], y_peer(d))
    send(xg.at[h], xg.at[h], xs_sem.at[0], xr_sem.at[h], sibling)
    send(mg.at[h], mg.at[h], ms_sem.at[0], mr_sem.at[h], sibling)
    send(wo.at[z, yh, x], wo.at[z, yh, x], wys_sem, wyr_sem, yh_peer)
    send(kvs.at[0], kvs.at[NX], ss_sem.at[0], sr_sem.at[NX], yh_peer)
    for d in range(1, NX):
        send(kvs.at[0], kvs.at[NX - d], ss_sem.at[d], sr_sem.at[NX - d], x_peer(d))

    for d in range(1, NYL):
        hs = ((yl + d) % NYL) * 2 + c
        arrived(xg.at[hs], xs_sem.at[d], xr_sem.at[hs], y_peer(d))
        arrived(mg.at[hs], ms_sem.at[d], mr_sem.at[hs], y_peer(d))
        send(xg.at[hs], xg.at[hs], xs_sem.at[NYL - 1 + d], xr_sem.at[hs], sibling)
        send(mg.at[hs], mg.at[hs], ms_sem.at[NYL - 1 + d], mr_sem.at[hs], sibling)

    arrived(wo.at[z, 1 - yh, x], wys_sem, wyr_sem, yh_peer)
    for d in (4, 3, 5, 2, 6, 1, 7):
        send(wo.at[z, :, x], wo.at[z, :, x], wzs_sem.at[d], wzr_sem.at[z], z_peer(d))
    arrived(kvs.at[NX], ss_sem.at[0], sr_sem.at[NX], yh_peer)
    for d in range(1, NX):
        send(kvs.at[NX], kvs.at[NX + NX - d], ss_sem.at[NX + d], sr_sem.at[NX + NX - d], x_peer(d))

    for d in range(NYL):
        hs = ((yl + d) % NYL) * 2 + 1 - c
        arrived(xg.at[hs], xs_sem.at[0], xr_sem.at[hs], sibling)
        arrived(mg.at[hs], ms_sem.at[0], mr_sem.at[hs], sibling)

    def forward_wo(d):
        zz = (z + d) % NZ
        if d:
            arrived(wo.at[zz, :, x], wzs_sem.at[d], wzr_sem.at[zz], z_peer(d))
        for e in range(1, NX):
            send(wo.at[zz, :, x], wo.at[zz, :, x], wxs_sem.at[d, e], wxr_sem.at[x, zz], x_peer(e))

    forward_wo(0)

    sum1 = jnp.zeros((2 * TOK, 128), F32)
    sum2 = jnp.zeros((2 * TOK, 128), F32)
    for j in range(8):
        v = xg[j].astype(F32)
        for k in range(FEAT // 128):
            part = v[:, k * 128 : (k + 1) * 128]
            sum1 += part
            sum2 += part * part
    mean = jnp.sum(sum1, axis=1, keepdims=True) / WIDTH
    square = jnp.sum(sum2, axis=1, keepdims=True) / WIDTH
    inv = lax.rsqrt(square - mean * mean + 1e-06)
    for j in range(8):
        v = (xg[j].astype(F32) - mean) * inv
        m = mg[j]
        for s in range(2):
            part = v[s * TOK : (s + 1) * TOK] * (1.0 + m[2 + s : 3 + s]) + m[s : s + 1]
            a_v[s * TOK : (s + 1) * TOK, j * FEAT : (j + 1) * FEAT] = part.astype(BF16)

    cos = jnp.concatenate([cos_ref[...]] * 2, axis=0)
    sin = jnp.concatenate([sin_ref[...]] * 2, axis=0)

    def rot(u):
        heads = []
        for i in range(2):
            uh = u[:, i * DH : (i + 1) * DH]
            heads.append(uh * cos + pltpu.roll(uh, DH // 2, 1) * sin)
        return jnp.concatenate(heads, axis=1).astype(BF16)

    loads[1].wait()
    kr = rot(dot_nn(a_v[...], w_v[1]))
    loads[2].wait()
    vr = dot_nn(a_v[...], w_v[2]).astype(BF16)
    kvf[0, 0] = kr[:TOK]
    kvf[0, 1] = vr[:TOK]
    kv1[0] = kr[TOK:]
    kv1[1] = vr[TOK:]
    send(kvf.at[0], kvf.at[NX], fs_sem.at[0], fr_sem.at[NX], yh_peer)
    for d in range(1, NX):
        send(kvf.at[0], kvf.at[NX - d], fs_sem.at[d], fr_sem.at[NX - d], x_peer(d))
    loads[0].wait()
    qb[0] = rot(dot_nn(a_v[...], w_v[0]))
    for d in (4, 3, 5, 2, 6, 1, 7):
        send(qb.at[0], qb.at[NZ - d], qs_sem.at[d], qr_sem.at[NZ - d], z_peer(d))

    arrived(kvf.at[NX], fs_sem.at[0], fr_sem.at[NX], yh_peer)
    for d in range(1, NX):
        send(kvf.at[NX], kvf.at[NX + NX - d], fs_sem.at[NX + d], fr_sem.at[NX + NX - d], x_peer(d))

    for d in (1, 7, 2, 6):
        forward_wo(d)

    inv_root = 1.0 / math.sqrt(DH)
    lane = lax.broadcasted_iota(jnp.int32, (NZ * TOK, 128), 1)
    ones = jnp.ones((NB * TOK, DH), BF16)

    def attend(s, held, own):
        outs, stats = [], jnp.zeros((NZ * TOK, 128), F32)
        for i in range(2):
            cols = slice(i * DH, (i + 1) * DH)
            keys = held[:, 0, :, cols].reshape(NB * TOK, DH)
            vals = held[:, 1, :, cols].reshape(NB * TOK, DH)
            own_keys = jnp.concatenate([own[0, :, cols], keys[TOK:]], axis=0)
            own_vals = jnp.concatenate([own[1, :, cols], vals[TOK:]], axis=0)
            q = qb[:, s * TOK : (s + 1) * TOK, cols].reshape(NZ * TOK, DH)
            scores = jnp.concatenate([dot_nt(q[:TOK], own_keys), dot_nt(q[TOK:], keys)], axis=0) * inv_root
            top = jnp.max(scores, axis=1, keepdims=True)
            weights = jnp.exp(scores - top).astype(BF16)
            mixed = jnp.concatenate(
                [
                    dot_nn(weights[:TOK], jnp.concatenate([own_vals, ones], axis=1)),
                    dot_nn(weights[TOK:], jnp.concatenate([vals, ones], axis=1)),
                ],
                axis=0,
            )
            total = mixed[:, DH:]
            outs.append((mixed[:, :DH] / total).astype(BF16))
            left = top + jnp.log(total)
            for k in range(3):
                piece = left.astype(BF16).astype(F32)
                stats = jnp.where(lane == 3 * i + k, piece, stats)
                left = left - piece
        full = jnp.concatenate(outs + [stats.astype(BF16)], axis=1).reshape(NZ, TOK, HC + 128)
        orc[s, 0] = full[0]
        for d in range(1, NZ):
            os_[s, d] = full[d]
        for d in (4, 3, 5, 2, 6, 1, 7):
            send(os_.at[s, d], orc.at[s, NZ - d], os_sem.at[s, d], or_sem.at[s, NZ - d], z_peer(d))

    for d in range(1, NX):
        arrived(kvs.at[d], ss_sem.at[d], sr_sem.at[d], x_peer(d))
        arrived(kvs.at[NX + d], ss_sem.at[NX + d], sr_sem.at[NX + d], x_peer(d))
    for d in range(1, NZ):
        arrived(qb.at[d], qs_sem.at[d], qr_sem.at[d], z_peer(d))
    attend(0, kvs, kvf.at[0])

    for d in (3, 5, 4):
        forward_wo(d)

    for d in range(1, NX):
        arrived(kvf.at[d], fs_sem.at[d], fr_sem.at[d], x_peer(d))
        arrived(kvf.at[NX + d], fs_sem.at[NX + d], fr_sem.at[NX + d], x_peer(d))
    attend(1, kvf, kv1)

    def merge(s):
        for d in range(1, NZ):
            arrived(orc.at[s, d], os_sem.at[s, d], or_sem.at[s, d], z_peer(d))
        heads = []
        for i in range(2):
            lse = []
            for d in range(NZ):
                st = orc[s, d, :, HC : HC + 128].astype(F32)
                k = 3 * i
                lse.append(st[:, k : k + 1] + st[:, k + 1 : k + 2] + st[:, k + 2 : k + 3])
            top = functools.reduce(jnp.maximum, lse)
            mixed = jnp.zeros((TOK, DH), F32)
            total = jnp.zeros((TOK, 1), F32)
            for d in range(NZ):
                weight = jnp.exp(lse[d] - top)
                total += weight
                mixed += weight * orc[s, d, :, i * DH : (i + 1) * DH].astype(F32)
            heads.append((mixed / total).astype(BF16))
        return jnp.concatenate(heads, axis=1)

    def block(o, j, core):
        return dot_nt(o, wo[((yl + j) % NYL) * 2 + core].reshape(FEAT, HC))

    def project(s):
        o = merge(s)
        if s == 0:
            for e in range(1, NX):
                for zz in range(NZ):
                    xs = (x + e) % NX
                    arrived(wo.at[zz, :, xs], wxs_sem.at[0, e], wxr_sem.at[xs, zz], x_peer(e))
        for j in (2, 1, 3, 0):
            e0s[s, j] = block(o, j, 1 - c).astype(BF16)
            send(e0s.at[s, j], e0r.at[s, j], e0s_sem.at[s, j], e0r_sem.at[s, j], sibling)
        for j in (2, 1, 3, 0):
            mine = block(o, j, c)
            arrived(e0r.at[s, j], e0s_sem.at[s, j], e0r_sem.at[s, j], sibling)
            mine = mine + e0r[s, j].astype(F32)
            if j:
                e1s[s, j] = mine.astype(BF16)
                send(e1s.at[s, j], e1r.at[s, NYL - j], e1s_sem.at[s, j], e1r_sem.at[s, NYL - j], y_peer(j))
            else:
                acc[s] = mine

    project(0)
    project(1)
    for s in range(2):
        total = acc[s]
        for j in range(1, NYL):
            arrived(e1r.at[s, j], e1s_sem.at[s, j], e1r_sem.at[s, j], y_peer(j))
            total = total + e1r[s, j].astype(F32)
        out_ref[s * TOK : (s + 1) * TOK] = (gates[s] * total).astype(BF16)

    for copy in sent:
        copy.wait_send()


def tables(slab_order):
    positions = slab_order[0] * TOK + jnp.arange(TOK, dtype=jnp.int32)
    half = DH // 2
    frequency = 10000.0 ** (-(2.0 * jnp.arange(half, dtype=F32)) / DH)
    angle = positions.astype(F32)[:, None] * frequency[None, :]
    cos, sin = jnp.cos(angle), jnp.sin(angle)
    return jnp.concatenate([cos, cos], axis=1), jnp.concatenate([-sin, sin], axis=1)


def body(inputs, stale_kv, w_qkv, w_out, mod_table, step_ids, slab_order):
    cos, sin = tables(slab_order)
    vmem = pl.BlockSpec(memory_space=pltpu.VMEM)
    dma = pltpu.SemaphoreType.DMA
    out = pl.pallas_call(
        kernel,
        out_shape=jax.ShapeDtypeStruct((2 * TOK, FEAT), BF16),
        in_specs=[
            vmem,
            vmem,
            pl.BlockSpec(memory_space=pl.ANY),
            vmem,
            vmem,
            pl.BlockSpec(memory_space=pltpu.SMEM),
            vmem,
            vmem,
        ],
        out_specs=vmem,
        scratch_shapes=[
            pltpu.VMEM((3, WIDTH, HC), BF16),
            pltpu.VMEM((8, 2 * TOK, FEAT), BF16),
            pltpu.VMEM((8, 4, FEAT), F32),
            pltpu.VMEM((2 * TOK, WIDTH), BF16),
            pltpu.VMEM((NB, 2, TOK, HC), BF16),
            pltpu.VMEM((NB, 2, TOK, HC), BF16),
            pltpu.VMEM((2, TOK, HC), BF16),
            pltpu.VMEM((NZ, 2 * TOK, HC), BF16),
            pltpu.VMEM((2, NZ, TOK, HC + 128), BF16),
            pltpu.VMEM((2, NZ, TOK, HC + 128), BF16),
            pltpu.VMEM((NZ, NYH, NX, OUTC, HC), BF16),
            pltpu.VMEM((2, NYL, TOK, FEAT), BF16),
            pltpu.VMEM((2, NYL, TOK, FEAT), BF16),
            pltpu.VMEM((2, NYL, TOK, FEAT), BF16),
            pltpu.VMEM((2, NYL, TOK, FEAT), BF16),
            pltpu.VMEM((2, TOK, FEAT), F32),
            dma((3,)),
            dma((7,)), dma((8,)), dma((7,)), dma((8,)),
            dma((8,)), dma((8,)), dma((8,)), dma((8,)),
            dma((8,)), dma((8,)), dma((2, 8)), dma((2, 8)),
            dma, dma, dma((8,)), dma((8,)), dma((8, 4)), dma((4, 8)),
            dma((2, 4)), dma((2, 4)), dma((2, 4)), dma((2, 4)),
        ],
        compiler_params=pltpu.CompilerParams(
            collective_id=0, has_side_effects=True, vmem_limit_bytes=40 * 1024 * 1024
        ),
        name="block",
    )(
        inputs.reshape(2 * TOK, FEAT),
        stale_kv,
        jnp.transpose(w_qkv, (1, 0, 2)),
        jnp.transpose(w_out),
        jnp.transpose(mod_table, (1, 0, 2)),
        step_ids,
        cos,
        sin,
    )
    return out.reshape(2, TOK, FEAT)


def solution(mesh):
    in_specs = (
        P(None, "patch", "head"),
        P(None, "patch", "head"),
        P(None, None, "head"),
        P("head", "patch"),
        P(None, None, "head"),
        P(),
        P("patch"),
    )
    out_specs = P(None, "patch", "head")
    return jax.shard_map(body, mesh=mesh, in_specs=in_specs, out_specs=out_specs, check_vma=False)
```

```python
import functools
import math

import jax
import jax.numpy as jnp
from jax import lax
from jax.experimental import pallas as pl
from jax.experimental.pallas import tpu as pltpu
from jax.sharding import PartitionSpec as P

DH = 128
TOK = 32
FEAT = 384
HC = 256
WIDTH = 3072
OUTC = 48
NZ, NYH, NX, NYL = 8, 2, 4, 4
NB = NYH * NX
F32 = jnp.float32
BF16 = jnp.bfloat16
MESH = pl.DeviceIdType.MESH


def dot_nt(a, b):
    return lax.dot_general(a, b, (((1,), (1,)), ((), ())), preferred_element_type=F32)


def dot_nn(a, b):
    return jnp.dot(a, b, preferred_element_type=F32)


def kernel(
    x_ref, stale_ref, w_ref, wo_ref, mod_ref, ids_ref, cos_ref, sin_ref, out_ref,
    ids_v, mod_v, w_v, xg, mg, a_v, kvs, kvf, kv1, qb, os_, orc, wo, e0s, e0r, e1s, e1r, acc,
    in_sem, w_sem, xs_sem, xr_sem, ms_sem, mr_sem,
    ss_sem, sr_sem, fs_sem, fr_sem, qs_sem, qr_sem, os_sem, or_sem,
    wys_sem, wyr_sem, wzs_sem, wzr_sem, wxs_sem, wxr_sem,
    e0s_sem, e0r_sem, e1s_sem, e1r_sem,
):
    p = lax.axis_index("patch")
    h = lax.axis_index("head")
    z, b = p // NB, p % NB
    yh, x = b // NX, b % NX
    yl, c = h // 2, h % 2

    def z_peer(d):
        return (((z + d) % NZ) * NB + b, h)

    def x_peer(d):
        return (z * NB + yh * NX + (x + d) % NX, h)

    yh_peer = (z * NB + (1 - yh) * NX + x, h)
    sibling = (p, yl * 2 + 1 - c)

    def y_peer(d):
        return (p, ((yl + d) % NYL) * 2 + c)

    peers = [sibling, yh_peer]
    peers += [y_peer(d) for d in range(1, NYL)]
    peers += [x_peer(d) for d in range(1, NX)]
    peers += [z_peer(d) for d in range(1, NZ)]

    barrier = pltpu.get_barrier_semaphore()
    for peer in peers:
        pl.semaphore_signal(barrier, inc=1, device_id=peer, device_id_type=MESH)

    sent = []

    def send(src, dst, ssem, rsem, peer):
        copy = pltpu.make_async_remote_copy(
            src_ref=src, dst_ref=dst, send_sem=ssem, recv_sem=rsem, device_id=peer, device_id_type=MESH
        )
        copy.start()
        sent.append(copy)

    def arrived(dst, ssem, rsem, peer):
        pltpu.make_async_remote_copy(
            src_ref=dst, dst_ref=dst, send_sem=ssem, recv_sem=rsem, device_id=peer, device_id_type=MESH
        ).wait_recv()

    small = [
        pltpu.make_async_copy(ids_ref, ids_v, in_sem.at[0]),
        pltpu.make_async_copy(mod_ref, mod_v, in_sem.at[1]),
        pltpu.make_async_copy(x_ref, xg.at[h], in_sem.at[2]),
        pltpu.make_async_copy(stale_ref, kvs.at[0], in_sem.at[3]),
        pltpu.make_async_copy(wo_ref, wo.at[z, yh, x], in_sem.at[4]),
    ]
    for load in small:
        load.start()
    loads = [pltpu.make_async_copy(w_ref.at[t], w_v.at[t], w_sem.at[t]) for t in range(3)]
    for t in (1, 2, 0):
        loads[t].start()
    small[0].wait()
    small[1].wait()

    table_row = lax.broadcasted_iota(jnp.int32, (4, FEAT), 0)
    gates = []
    for s in range(2):
        pick = table_row == ids_v[s]
        rows = [jnp.sum(jnp.where(pick, mod_v[k], 0.0), axis=0, keepdims=True) for k in range(3)]
        mg[h, s : s + 1] = rows[0]
        mg[h, 2 + s : 3 + s] = rows[1]
        gates.append(rows[2])
    for load in small[2:]:
        load.wait()

    pl.semaphore_wait(barrier, len(peers))

    for d in (2, 1, 3):
        send(xg.at[h], xg.at[h], xs_sem.at[d], xr_sem.at[h], y_peer(d))
        send(mg.at[h], mg.at[h], ms_sem.at[d], mr_sem.at[h], y_peer(d))
    send(xg.at[h], xg.at[h], xs_sem.at[0], xr_sem.at[h], sibling)
    send(mg.at[h], mg.at[h], ms_sem.at[0], mr_sem.at[h], sibling)
    send(wo.at[z, yh, x], wo.at[z, yh, x], wys_sem, wyr_sem, yh_peer)
    send(kvs.at[0], kvs.at[NX], ss_sem.at[0], sr_sem.at[NX], yh_peer)
    for d in range(1, NX):
        send(kvs.at[0], kvs.at[NX - d], ss_sem.at[d], sr_sem.at[NX - d], x_peer(d))

    for d in range(1, NYL):
        hs = ((yl + d) % NYL) * 2 + c
        arrived(xg.at[hs], xs_sem.at[d], xr_sem.at[hs], y_peer(d))
        arrived(mg.at[hs], ms_sem.at[d], mr_sem.at[hs], y_peer(d))
        send(xg.at[hs], xg.at[hs], xs_sem.at[NYL - 1 + d], xr_sem.at[hs], sibling)
        send(mg.at[hs], mg.at[hs], ms_sem.at[NYL - 1 + d], mr_sem.at[hs], sibling)

    arrived(wo.at[z, 1 - yh, x], wys_sem, wyr_sem, yh_peer)
    for d in (4, 3, 5, 2, 6, 1, 7):
        send(wo.at[z, :, x], wo.at[z, :, x], wzs_sem.at[d], wzr_sem.at[z], z_peer(d))
    arrived(kvs.at[NX], ss_sem.at[0], sr_sem.at[NX], yh_peer)
    for d in range(1, NX):
        send(kvs.at[NX], kvs.at[NX + NX - d], ss_sem.at[NX + d], sr_sem.at[NX + NX - d], x_peer(d))

    for d in range(NYL):
        hs = ((yl + d) % NYL) * 2 + 1 - c
        arrived(xg.at[hs], xs_sem.at[0], xr_sem.at[hs], sibling)
        arrived(mg.at[hs], ms_sem.at[0], mr_sem.at[hs], sibling)

    def forward_wo(d):
        zz = (z + d) % NZ
        if d:
            arrived(wo.at[zz, :, x], wzs_sem.at[d], wzr_sem.at[zz], z_peer(d))
        for e in range(1, NX):
            send(wo.at[zz, :, x], wo.at[zz, :, x], wxs_sem.at[d, e], wxr_sem.at[x, zz], x_peer(e))

    forward_wo(0)

    sum1 = jnp.zeros((2 * TOK, 128), F32)
    sum2 = jnp.zeros((2 * TOK, 128), F32)
    for j in range(8):
        v = xg[j].astype(F32)
        for k in range(FEAT // 128):
            part = v[:, k * 128 : (k + 1) * 128]
            sum1 += part
            sum2 += part * part
    mean = jnp.sum(sum1, axis=1, keepdims=True) / WIDTH
    square = jnp.sum(sum2, axis=1, keepdims=True) / WIDTH
    inv = lax.rsqrt(square - mean * mean + 1e-06)
    for j in range(8):
        v = (xg[j].astype(F32) - mean) * inv
        m = mg[j]
        for s in range(2):
            part = v[s * TOK : (s + 1) * TOK] * (1.0 + m[2 + s : 3 + s]) + m[s : s + 1]
            a_v[s * TOK : (s + 1) * TOK, j * FEAT : (j + 1) * FEAT] = part.astype(BF16)

    cos = jnp.concatenate([cos_ref[...]] * 2, axis=0)
    sin = jnp.concatenate([sin_ref[...]] * 2, axis=0)

    def rot(u):
        heads = []
        for i in range(2):
            uh = u[:, i * DH : (i + 1) * DH]
            heads.append(uh * cos + pltpu.roll(uh, DH // 2, 1) * sin)
        return jnp.concatenate(heads, axis=1).astype(BF16)

    loads[1].wait()
    kr = rot(dot_nn(a_v[...], w_v[1]))
    loads[2].wait()
    vr = dot_nn(a_v[...], w_v[2]).astype(BF16)
    kvf[0, 0] = kr[:TOK]
    kvf[0, 1] = vr[:TOK]
    kv1[0] = kr[TOK:]
    kv1[1] = vr[TOK:]
    send(kvf.at[0], kvf.at[NX], fs_sem.at[0], fr_sem.at[NX], yh_peer)
    for d in range(1, NX):
        send(kvf.at[0], kvf.at[NX - d], fs_sem.at[d], fr_sem.at[NX - d], x_peer(d))
    loads[0].wait()
    qb[0] = rot(dot_nn(a_v[...], w_v[0]))
    for d in (4, 3, 5, 2, 6, 1, 7):
        send(qb.at[0], qb.at[NZ - d], qs_sem.at[d], qr_sem.at[NZ - d], z_peer(d))

    arrived(kvf.at[NX], fs_sem.at[0], fr_sem.at[NX], yh_peer)
    for d in range(1, NX):
        send(kvf.at[NX], kvf.at[NX + NX - d], fs_sem.at[NX + d], fr_sem.at[NX + NX - d], x_peer(d))

    for d in (1, 7, 2, 6):
        forward_wo(d)

    inv_root = 1.0 / math.sqrt(DH)
    lane = lax.broadcasted_iota(jnp.int32, (NZ * TOK, 128), 1)
    ones = jnp.ones((NB * TOK, DH), BF16)

    def attend(s, held, own):
        outs, stats = [], jnp.zeros((NZ * TOK, 128), F32)
        for i in range(2):
            cols = slice(i * DH, (i + 1) * DH)
            keys = held[:, 0, :, cols].reshape(NB * TOK, DH)
            vals = held[:, 1, :, cols].reshape(NB * TOK, DH)
            own_keys = jnp.concatenate([own[0, :, cols], keys[TOK:]], axis=0)
            own_vals = jnp.concatenate([own[1, :, cols], vals[TOK:]], axis=0)
            q = qb[:, s * TOK : (s + 1) * TOK, cols].reshape(NZ * TOK, DH)
            scores = jnp.concatenate([dot_nt(q[:TOK], own_keys), dot_nt(q[TOK:], keys)], axis=0) * inv_root
            top = jnp.max(scores, axis=1, keepdims=True)
            weights = jnp.exp(scores - top).astype(BF16)
            mixed = jnp.concatenate(
                [
                    dot_nn(weights[:TOK], jnp.concatenate([own_vals, ones], axis=1)),
                    dot_nn(weights[TOK:], jnp.concatenate([vals, ones], axis=1)),
                ],
                axis=0,
            )
            total = mixed[:, DH:]
            outs.append((mixed[:, :DH] / total).astype(BF16))
            left = top + jnp.log(total)
            for k in range(3):
                piece = left.astype(BF16).astype(F32)
                stats = jnp.where(lane == 3 * i + k, piece, stats)
                left = left - piece
        full = jnp.concatenate(outs + [stats.astype(BF16)], axis=1).reshape(NZ, TOK, HC + 128)
        orc[s, 0] = full[0]
        for d in range(1, NZ):
            os_[s, d] = full[d]
        for d in (4, 3, 5, 2, 6, 1, 7):
            send(os_.at[s, d], orc.at[s, NZ - d], os_sem.at[s, d], or_sem.at[s, NZ - d], z_peer(d))

    for d in range(1, NX):
        arrived(kvs.at[d], ss_sem.at[d], sr_sem.at[d], x_peer(d))
        arrived(kvs.at[NX + d], ss_sem.at[NX + d], sr_sem.at[NX + d], x_peer(d))
    for d in range(1, NZ):
        arrived(qb.at[d], qs_sem.at[d], qr_sem.at[d], z_peer(d))
    attend(0, kvs, kvf.at[0])

    for d in (3, 5, 4):
        forward_wo(d)

    for d in range(1, NX):
        arrived(kvf.at[d], fs_sem.at[d], fr_sem.at[d], x_peer(d))
        arrived(kvf.at[NX + d], fs_sem.at[NX + d], fr_sem.at[NX + d], x_peer(d))
    attend(1, kvf, kv1)

    def merge(s):
        for d in range(1, NZ):
            arrived(orc.at[s, d], os_sem.at[s, d], or_sem.at[s, d], z_peer(d))
        heads = []
        for i in range(2):
            lse = []
            for d in range(NZ):
                st = orc[s, d, :, HC : HC + 128].astype(F32)
                k = 3 * i
                lse.append(st[:, k : k + 1] + st[:, k + 1 : k + 2] + st[:, k + 2 : k + 3])
            top = functools.reduce(jnp.maximum, lse)
            mixed = jnp.zeros((TOK, DH), F32)
            total = jnp.zeros((TOK, 1), F32)
            for d in range(NZ):
                weight = jnp.exp(lse[d] - top)
                total += weight
                mixed += weight * orc[s, d, :, i * DH : (i + 1) * DH].astype(F32)
            heads.append((mixed / total).astype(BF16))
        return jnp.concatenate(heads, axis=1)

    def block(o, j, core):
        return dot_nt(o, wo[((yl + j) % NYL) * 2 + core].reshape(FEAT, HC))

    def project(s):
        o = merge(s)
        if s == 0:
            for e in range(1, NX):
                for zz in range(NZ):
                    xs = (x + e) % NX
                    arrived(wo.at[zz, :, xs], wxs_sem.at[0, e], wxr_sem.at[xs, zz], x_peer(e))
        for j in (2, 1, 3, 0):
            e0s[s, j] = block(o, j, 1 - c).astype(BF16)
            send(e0s.at[s, j], e0r.at[s, j], e0s_sem.at[s, j], e0r_sem.at[s, j], sibling)
        for j in (2, 1, 3, 0):
            mine = block(o, j, c)
            arrived(e0r.at[s, j], e0s_sem.at[s, j], e0r_sem.at[s, j], sibling)
            mine = mine + e0r[s, j].astype(F32)
            if j:
                e1s[s, j] = mine.astype(BF16)
                send(e1s.at[s, j], e1r.at[s, NYL - j], e1s_sem.at[s, j], e1r_sem.at[s, NYL - j], y_peer(j))
            else:
                acc[s] = mine

    project(0)
    project(1)
    for s in range(2):
        total = acc[s]
        for j in range(1, NYL):
            arrived(e1r.at[s, j], e1s_sem.at[s, j], e1r_sem.at[s, j], y_peer(j))
            total = total + e1r[s, j].astype(F32)
        out_ref[s * TOK : (s + 1) * TOK] = (gates[s] * total).astype(BF16)

    for copy in sent:
        copy.wait_send()


def tables(slab_order):
    positions = slab_order[0] * TOK + jnp.arange(TOK, dtype=jnp.int32)
    half = DH // 2
    frequency = 10000.0 ** (-(2.0 * jnp.arange(half, dtype=F32)) / DH)
    angle = positions.astype(F32)[:, None] * frequency[None, :]
    cos, sin = jnp.cos(angle), jnp.sin(angle)
    return jnp.concatenate([cos, cos], axis=1), jnp.concatenate([-sin, sin], axis=1)


def body(inputs, stale_kv, w_qkv, w_out, mod_table, step_ids, slab_order):
    cos, sin = tables(slab_order)
    vmem = pl.BlockSpec(memory_space=pltpu.VMEM)
    dma = pltpu.SemaphoreType.DMA
    out = pl.pallas_call(
        kernel,
        out_shape=jax.ShapeDtypeStruct((2 * TOK, FEAT), BF16),
        in_specs=[pl.BlockSpec(memory_space=pltpu.HBM)] * 6 + [vmem] * 2,
        out_specs=vmem,
        scratch_shapes=[
            pltpu.SMEM((2,), jnp.int32),
            pltpu.VMEM((3, 4, FEAT), F32),
            pltpu.VMEM((3, WIDTH, HC), BF16),
            pltpu.VMEM((8, 2 * TOK, FEAT), BF16),
            pltpu.VMEM((8, 4, FEAT), F32),
            pltpu.VMEM((2 * TOK, WIDTH), BF16),
            pltpu.VMEM((NB, 2, TOK, HC), BF16),
            pltpu.VMEM((NB, 2, TOK, HC), BF16),
            pltpu.VMEM((2, TOK, HC), BF16),
            pltpu.VMEM((NZ, 2 * TOK, HC), BF16),
            pltpu.VMEM((2, NZ, TOK, HC + 128), BF16),
            pltpu.VMEM((2, NZ, TOK, HC + 128), BF16),
            pltpu.VMEM((NZ, NYH, NX, OUTC, HC), BF16),
            pltpu.VMEM((2, NYL, TOK, FEAT), BF16),
            pltpu.VMEM((2, NYL, TOK, FEAT), BF16),
            pltpu.VMEM((2, NYL, TOK, FEAT), BF16),
            pltpu.VMEM((2, NYL, TOK, FEAT), BF16),
            pltpu.VMEM((2, TOK, FEAT), F32),
            dma((5,)), dma((3,)),
            dma((7,)), dma((8,)), dma((7,)), dma((8,)),
            dma((8,)), dma((8,)), dma((8,)), dma((8,)),
            dma((8,)), dma((8,)), dma((2, 8)), dma((2, 8)),
            dma, dma, dma((8,)), dma((8,)), dma((8, 4)), dma((4, 8)),
            dma((2, 4)), dma((2, 4)), dma((2, 4)), dma((2, 4)),
        ],
        compiler_params=pltpu.CompilerParams(
            collective_id=0, has_side_effects=True, vmem_limit_bytes=60 * 1024 * 1024
        ),
        name="block",
    )(
        inputs.reshape(2 * TOK, FEAT),
        stale_kv,
        jnp.transpose(w_qkv, (1, 0, 2)),
        jnp.transpose(w_out),
        jnp.transpose(mod_table, (1, 0, 2)),
        step_ids,
        cos,
        sin,
    )
    return out.reshape(2, TOK, FEAT)


def solution(mesh):
    in_specs = (
        P(None, "patch", "head"),
        P(None, "patch", "head"),
        P(None, None, "head"),
        P("head", "patch"),
        P(None, None, "head"),
        P(),
        P("patch"),
    )
    out_specs = P(None, "patch", "head")
    return jax.shard_map(body, mesh=mesh, in_specs=in_specs, out_specs=out_specs, check_vma=False)
```

```python
import functools
import math

import jax
import jax.numpy as jnp
from jax import lax
from jax.experimental import pallas as pl
from jax.experimental.pallas import tpu as pltpu
from jax.sharding import PartitionSpec as P

DH = 128
TOK = 32
FEAT = 384
HC = 256
WIDTH = 3072
OUTC = 48
NZ, NYH, NX, NYL = 8, 2, 4, 4
NB = NYH * NX
NK = NYH * NZ
NEAR = (1, NZ - 1, 2, NZ - 2)
F32 = jnp.float32
BF16 = jnp.bfloat16
MESH = pl.DeviceIdType.MESH


def dot_nt(a, b):
    return lax.dot_general(a, b, (((1,), (1,)), ((), ())), preferred_element_type=F32)


def dot_nn(a, b):
    return jnp.dot(a, b, preferred_element_type=F32)


def kernel(
    x_ref, stale_ref, w_ref, wo_ref, mod_ref, ids_ref, cos_ref, sin_ref, out_ref,
    ids_v, mod_v, w_v, xg, mg, a_v, kvs, kvf, kv1, qb, os_, orc, wo, e0s, e0r, e1s, e1r, acc,
    in_sem, w_sem, xs_sem, xr_sem, ms_sem, mr_sem,
    ss_sem, sr_sem, fs_sem, fr_sem, qs_sem, qr_sem, os_sem, or_sem,
    wys_sem, wyr_sem, wzs_sem, wzr_sem, wxs_sem, wxr_sem,
    e0s_sem, e0r_sem, e1s_sem, e1r_sem,
):
    p = lax.axis_index("patch")
    h = lax.axis_index("head")
    z, b = p // NB, p % NB
    yh, x = b // NX, b % NX
    yl, c = h // 2, h % 2

    def z_peer(d):
        return (((z + d % NZ) % NZ) * NB + b, h)

    def x_peer(d):
        return (z * NB + yh * NX + (x + d) % NX, h)

    yh_peer = (z * NB + (1 - yh) * NX + x, h)
    sibling = (p, yl * 2 + 1 - c)

    def y_peer(d):
        return (p, ((yl + d) % NYL) * 2 + c)

    peers = [sibling, yh_peer]
    peers += [y_peer(d) for d in range(1, NYL)]
    peers += [x_peer(d) for d in range(1, NX)]
    peers += [z_peer(d) for d in NEAR]

    barrier = pltpu.get_barrier_semaphore()
    for peer in peers:
        pl.semaphore_signal(barrier, inc=1, device_id=peer, device_id_type=MESH)

    sent = []

    def send(src, dst, ssem, rsem, peer):
        copy = pltpu.make_async_remote_copy(
            src_ref=src, dst_ref=dst, send_sem=ssem, recv_sem=rsem, device_id=peer, device_id_type=MESH
        )
        copy.start()
        sent.append(copy)

    def arrived(dst, ssem, rsem, peer):
        pltpu.make_async_remote_copy(
            src_ref=dst, dst_ref=dst, send_sem=ssem, recv_sem=rsem, device_id=peer, device_id_type=MESH
        ).wait_recv()

    small = [
        pltpu.make_async_copy(ids_ref, ids_v, in_sem.at[0]),
        pltpu.make_async_copy(mod_ref, mod_v, in_sem.at[1]),
        pltpu.make_async_copy(x_ref, xg.at[h], in_sem.at[2]),
        pltpu.make_async_copy(stale_ref, kvs.at[0], in_sem.at[3]),
        pltpu.make_async_copy(wo_ref, wo.at[z, yh, x], in_sem.at[4]),
    ]
    for load in small:
        load.start()
    loads = [pltpu.make_async_copy(w_ref.at[t], w_v.at[t], w_sem.at[t]) for t in range(3)]
    for t in (1, 2, 0):
        loads[t].start()
    small[0].wait()
    small[1].wait()

    table_row = lax.broadcasted_iota(jnp.int32, (4, FEAT), 0)
    gates = []
    for s in range(2):
        pick = table_row == ids_v[s]
        rows = [jnp.sum(jnp.where(pick, mod_v[k], 0.0), axis=0, keepdims=True) for k in range(3)]
        mg[h, s : s + 1] = rows[0]
        mg[h, 2 + s : 3 + s] = rows[1]
        gates.append(rows[2])
    for load in small[2:]:
        load.wait()

    pl.semaphore_wait(barrier, len(peers))

    for d in (2, 1, 3):
        send(xg.at[h], xg.at[h], xs_sem.at[d], xr_sem.at[h], y_peer(d))
        send(mg.at[h], mg.at[h], ms_sem.at[d], mr_sem.at[h], y_peer(d))
    send(xg.at[h], xg.at[h], xs_sem.at[0], xr_sem.at[h], sibling)
    send(mg.at[h], mg.at[h], ms_sem.at[0], mr_sem.at[h], sibling)

    def kv_near(buf, ssem, rsem, yrel):
        base = yrel * NZ
        for d in NEAR:
            send(buf.at[base], buf.at[base + NZ - d], ssem.at[base + d], rsem.at[base + NZ - d], z_peer(d))

    def kv_partner(buf, ssem, rsem):
        send(buf.at[0], buf.at[NZ], ssem.at[0], rsem.at[NZ], yh_peer)

    def kv_from_partner(buf, ssem, rsem):
        arrived(buf.at[NZ], ssem.at[0], rsem.at[NZ], yh_peer)
        kv_near(buf, ssem, rsem, 1)

    def kv_far(buf, ssem, rsem, yrel):
        base = yrel * NZ
        arrived(buf.at[base + 2], ssem.at[base + 2], rsem.at[base + 2], z_peer(2))
        send(buf.at[base + 2], buf.at[base + 3], ssem.at[base + 3], rsem.at[base + 3], z_peer(-1))
        send(buf.at[base + 2, 0], buf.at[base + 4, 0], ssem.at[base + 4], rsem.at[base + 4], z_peer(-2))
        arrived(buf.at[base + 6], ssem.at[base + 6], rsem.at[base + 6], z_peer(-2))
        send(buf.at[base + 6], buf.at[base + 5], ssem.at[base + 5], rsem.at[base + 5], z_peer(1))
        send(buf.at[base + 6, 1], buf.at[base + 4, 1], ssem.at[NK + yrel], rsem.at[NK + yrel], z_peer(2))

    def kv_all(buf, ssem, rsem):
        for yrel in range(NYH):
            base = yrel * NZ
            for d in (1, 7):
                arrived(buf.at[base + d], ssem.at[base + d], rsem.at[base + d], z_peer(d))
            arrived(buf.at[base + 3], ssem.at[base + 3], rsem.at[base + 3], z_peer(1))
            arrived(buf.at[base + 5], ssem.at[base + 5], rsem.at[base + 5], z_peer(-1))
            arrived(buf.at[base + 4, 0], ssem.at[base + 4], rsem.at[base + 4], z_peer(2))
            arrived(buf.at[base + 4, 1], ssem.at[NK + yrel], rsem.at[NK + yrel], z_peer(-2))

    def wo_near():
        arrived(wo.at[z, 1 - yh, x], wys_sem, wyr_sem, yh_peer)
        for d in NEAR:
            send(wo.at[z, :, x], wo.at[z, :, x], wzs_sem.at[d], wzr_sem.at[z], z_peer(d))

    def wo_take(d):
        zz = (z + d) % NZ
        if d == 4:
            arrived(wo.at[zz, 0, x], wzs_sem.at[4], wzr_sem.at[zz], z_peer(2))
            arrived(wo.at[zz, 1, x], wzs_sem.at[0], wzr_sem.at[NZ], z_peer(-2))
        elif d:
            arrived(wo.at[zz, :, x], wzs_sem.at[d], wzr_sem.at[zz], z_peer(d))
        if d == 2:
            send(wo.at[zz, :, x], wo.at[zz, :, x], wzs_sem.at[3], wzr_sem.at[zz], z_peer(-1))
            send(wo.at[zz, 0, x], wo.at[zz, 0, x], wzs_sem.at[4], wzr_sem.at[zz], z_peer(-2))
        if d == 6:
            send(wo.at[zz, :, x], wo.at[zz, :, x], wzs_sem.at[5], wzr_sem.at[zz], z_peer(1))
            send(wo.at[zz, 1, x], wo.at[zz, 1, x], wzs_sem.at[0], wzr_sem.at[NZ], z_peer(2))
        for e in range(1, NX):
            send(wo.at[zz, :, x], wo.at[zz, :, x], wxs_sem.at[d, e], wxr_sem.at[x, zz], x_peer(e))

    kv_near(kvs, ss_sem, sr_sem, 0)
    kv_partner(kvs, ss_sem, sr_sem)
    send(wo.at[z, yh, x], wo.at[z, yh, x], wys_sem, wyr_sem, yh_peer)

    for d in range(1, NYL):
        hs = ((yl + d) % NYL) * 2 + c
        arrived(xg.at[hs], xs_sem.at[d], xr_sem.at[hs], y_peer(d))
        arrived(mg.at[hs], ms_sem.at[d], mr_sem.at[hs], y_peer(d))
        send(xg.at[hs], xg.at[hs], xs_sem.at[NYL - 1 + d], xr_sem.at[hs], sibling)
        send(mg.at[hs], mg.at[hs], ms_sem.at[NYL - 1 + d], mr_sem.at[hs], sibling)

    kv_from_partner(kvs, ss_sem, sr_sem)
    kv_far(kvs, ss_sem, sr_sem, 0)
    wo_near()
    wo_take(0)

    for d in range(NYL):
        hs = ((yl + d) % NYL) * 2 + 1 - c
        arrived(xg.at[hs], xs_sem.at[0], xr_sem.at[hs], sibling)
        arrived(mg.at[hs], ms_sem.at[0], mr_sem.at[hs], sibling)

    sum1 = jnp.zeros((2 * TOK, 128), F32)
    sum2 = jnp.zeros((2 * TOK, 128), F32)
    for j in range(8):
        v = xg[j].astype(F32)
        for k in range(FEAT // 128):
            part = v[:, k * 128 : (k + 1) * 128]
            sum1 += part
            sum2 += part * part
    mean = jnp.sum(sum1, axis=1, keepdims=True) / WIDTH
    square = jnp.sum(sum2, axis=1, keepdims=True) / WIDTH
    inv = lax.rsqrt(square - mean * mean + 1e-06)
    for j in range(8):
        v = (xg[j].astype(F32) - mean) * inv
        m = mg[j]
        for s in range(2):
            part = v[s * TOK : (s + 1) * TOK] * (1.0 + m[2 + s : 3 + s]) + m[s : s + 1]
            a_v[s * TOK : (s + 1) * TOK, j * FEAT : (j + 1) * FEAT] = part.astype(BF16)

    cos = jnp.concatenate([cos_ref[...]] * 2, axis=0)
    sin = jnp.concatenate([sin_ref[...]] * 2, axis=0)

    def rot(u):
        heads = []
        for i in range(2):
            uh = u[:, i * DH : (i + 1) * DH]
            heads.append(uh * cos + pltpu.roll(uh, DH // 2, 1) * sin)
        return jnp.concatenate(heads, axis=1).astype(BF16)

    loads[1].wait()
    kr = rot(dot_nn(a_v[...], w_v[1]))
    loads[2].wait()
    vr = dot_nn(a_v[...], w_v[2]).astype(BF16)
    kvf[0, 0] = kr[:TOK]
    kvf[0, 1] = vr[:TOK]
    kv1[0] = kr[TOK:]
    kv1[1] = vr[TOK:]
    kv_near(kvf, fs_sem, fr_sem, 0)
    kv_partner(kvf, fs_sem, fr_sem)
    loads[0].wait()
    qb[0] = rot(dot_nn(a_v[...], w_v[0]))
    for d in (2, 1, 3):
        send(qb.at[0], qb.at[NX - d], qs_sem.at[d], qr_sem.at[NX - d], x_peer(d))

    kv_far(kvs, ss_sem, sr_sem, 1)
    wo_take(2)
    wo_take(6)
    kv_far(kvf, fs_sem, fr_sem, 0)
    kv_from_partner(kvf, fs_sem, fr_sem)
    wo_take(1)
    wo_take(7)

    inv_root = 1.0 / math.sqrt(DH)
    lane = lax.broadcasted_iota(jnp.int32, (NX * TOK, 128), 1)
    ones = jnp.ones((NK * TOK, DH), BF16)

    def attend(s, held, own):
        outs, stats = [], jnp.zeros((NX * TOK, 128), F32)
        for i in range(2):
            cols = slice(i * DH, (i + 1) * DH)
            keys = held[:, 0, :, cols].reshape(NK * TOK, DH)
            vals = held[:, 1, :, cols].reshape(NK * TOK, DH)
            own_keys = jnp.concatenate([own[0, :, cols], keys[TOK:]], axis=0)
            own_vals = jnp.concatenate([own[1, :, cols], vals[TOK:]], axis=0)
            q = qb[:, s * TOK : (s + 1) * TOK, cols].reshape(NX * TOK, DH)
            scores = jnp.concatenate([dot_nt(q[:TOK], own_keys), dot_nt(q[TOK:], keys)], axis=0) * inv_root
            top = jnp.max(scores, axis=1, keepdims=True)
            weights = jnp.exp(scores - top).astype(BF16)
            mixed = jnp.concatenate(
                [
                    dot_nn(weights[:TOK], jnp.concatenate([own_vals, ones], axis=1)),
                    dot_nn(weights[TOK:], jnp.concatenate([vals, ones], axis=1)),
                ],
                axis=0,
            )
            total = mixed[:, DH:]
            outs.append((mixed[:, :DH] / total).astype(BF16))
            left = top + jnp.log(total)
            for k in range(3):
                piece = left.astype(BF16).astype(F32)
                stats = jnp.where(lane == 3 * i + k, piece, stats)
                left = left - piece
        full = jnp.concatenate(outs + [stats.astype(BF16)], axis=1).reshape(NX, TOK, HC + 128)
        orc[s, 0] = full[0]
        for d in range(1, NX):
            os_[s, d] = full[d]
        for d in (2, 1, 3):
            send(os_.at[s, d], orc.at[s, NX - d], os_sem.at[s, d], or_sem.at[s, NX - d], x_peer(d))

    kv_all(kvs, ss_sem, sr_sem)
    for d in range(1, NX):
        arrived(qb.at[d], qs_sem.at[d], qr_sem.at[d], x_peer(d))
    attend(0, kvs, kvf.at[0])

    kv_far(kvf, fs_sem, fr_sem, 1)
    for d in (3, 5, 4):
        wo_take(d)

    kv_all(kvf, fs_sem, fr_sem)
    attend(1, kvf, kv1)

    def merge(s):
        for d in range(1, NX):
            arrived(orc.at[s, d], os_sem.at[s, d], or_sem.at[s, d], x_peer(d))
        heads = []
        for i in range(2):
            lse = []
            for d in range(NX):
                st = orc[s, d, :, HC : HC + 128].astype(F32)
                k = 3 * i
                lse.append(st[:, k : k + 1] + st[:, k + 1 : k + 2] + st[:, k + 2 : k + 3])
            top = functools.reduce(jnp.maximum, lse)
            mixed = jnp.zeros((TOK, DH), F32)
            total = jnp.zeros((TOK, 1), F32)
            for d in range(NX):
                weight = jnp.exp(lse[d] - top)
                total += weight
                mixed += weight * orc[s, d, :, i * DH : (i + 1) * DH].astype(F32)
            heads.append((mixed / total).astype(BF16))
        return jnp.concatenate(heads, axis=1)

    def block(o, j, core):
        return dot_nt(o, wo[((yl + j) % NYL) * 2 + core].reshape(FEAT, HC))

    def project(s):
        o = merge(s)
        if s == 0:
            for e in range(1, NX):
                for zz in range(NZ):
                    xs = (x + e) % NX
                    arrived(wo.at[zz, :, xs], wxs_sem.at[0, e], wxr_sem.at[xs, zz], x_peer(e))
        for j in (2, 1, 3, 0):
            e0s[s, j] = block(o, j, 1 - c).astype(BF16)
            send(e0s.at[s, j], e0r.at[s, j], e0s_sem.at[s, j], e0r_sem.at[s, j], sibling)
        for j in (2, 1, 3, 0):
            mine = block(o, j, c)
            arrived(e0r.at[s, j], e0s_sem.at[s, j], e0r_sem.at[s, j], sibling)
            mine = mine + e0r[s, j].astype(F32)
            if j:
                e1s[s, j] = mine.astype(BF16)
                send(e1s.at[s, j], e1r.at[s, NYL - j], e1s_sem.at[s, j], e1r_sem.at[s, NYL - j], y_peer(j))
            else:
                acc[s] = mine

    project(0)
    project(1)
    for s in range(2):
        total = acc[s]
        for j in range(1, NYL):
            arrived(e1r.at[s, j], e1s_sem.at[s, j], e1r_sem.at[s, j], y_peer(j))
            total = total + e1r[s, j].astype(F32)
        out_ref[s * TOK : (s + 1) * TOK] = (gates[s] * total).astype(BF16)

    for copy in sent:
        copy.wait_send()


def tables(slab_order):
    positions = slab_order[0] * TOK + jnp.arange(TOK, dtype=jnp.int32)
    half = DH // 2
    frequency = 10000.0 ** (-(2.0 * jnp.arange(half, dtype=F32)) / DH)
    angle = positions.astype(F32)[:, None] * frequency[None, :]
    cos, sin = jnp.cos(angle), jnp.sin(angle)
    return jnp.concatenate([cos, cos], axis=1), jnp.concatenate([-sin, sin], axis=1)


def body(inputs, stale_kv, w_qkv, w_out, mod_table, step_ids, slab_order):
    cos, sin = tables(slab_order)
    vmem = pl.BlockSpec(memory_space=pltpu.VMEM)
    dma = pltpu.SemaphoreType.DMA
    out = pl.pallas_call(
        kernel,
        out_shape=jax.ShapeDtypeStruct((2 * TOK, FEAT), BF16),
        in_specs=[pl.BlockSpec(memory_space=pltpu.HBM)] * 6 + [vmem] * 2,
        out_specs=vmem,
        scratch_shapes=[
            pltpu.SMEM((2,), jnp.int32),
            pltpu.VMEM((3, 4, FEAT), F32),
            pltpu.VMEM((3, WIDTH, HC), BF16),
            pltpu.VMEM((8, 2 * TOK, FEAT), BF16),
            pltpu.VMEM((8, 4, FEAT), F32),
            pltpu.VMEM((2 * TOK, WIDTH), BF16),
            pltpu.VMEM((NK, 2, TOK, HC), BF16),
            pltpu.VMEM((NK, 2, TOK, HC), BF16),
            pltpu.VMEM((2, TOK, HC), BF16),
            pltpu.VMEM((NX, 2 * TOK, HC), BF16),
            pltpu.VMEM((2, NX, TOK, HC + 128), BF16),
            pltpu.VMEM((2, NX, TOK, HC + 128), BF16),
            pltpu.VMEM((NZ, NYH, NX, OUTC, HC), BF16),
            pltpu.VMEM((2, NYL, TOK, FEAT), BF16),
            pltpu.VMEM((2, NYL, TOK, FEAT), BF16),
            pltpu.VMEM((2, NYL, TOK, FEAT), BF16),
            pltpu.VMEM((2, NYL, TOK, FEAT), BF16),
            pltpu.VMEM((2, TOK, FEAT), F32),
            dma((5,)), dma((3,)),
            dma((7,)), dma((8,)), dma((7,)), dma((8,)),
            dma((18,)), dma((18,)), dma((18,)), dma((18,)),
            dma((4,)), dma((4,)), dma((2, 4)), dma((2, 4)),
            dma, dma, dma((8,)), dma((9,)), dma((8, 4)), dma((4, 8)),
            dma((2, 4)), dma((2, 4)), dma((2, 4)), dma((2, 4)),
        ],
        compiler_params=pltpu.CompilerParams(
            collective_id=0, has_side_effects=True, vmem_limit_bytes=60 * 1024 * 1024
        ),
        name="block",
    )(
        inputs.reshape(2 * TOK, FEAT),
        stale_kv,
        jnp.transpose(w_qkv, (1, 0, 2)),
        jnp.transpose(w_out),
        jnp.transpose(mod_table, (1, 0, 2)),
        step_ids,
        cos,
        sin,
    )
    return out.reshape(2, TOK, FEAT)


def solution(mesh):
    in_specs = (
        P(None, "patch", "head"),
        P(None, "patch", "head"),
        P(None, None, "head"),
        P("head", "patch"),
        P(None, None, "head"),
        P(),
        P("patch"),
    )
    out_specs = P(None, "patch", "head")
    return jax.shard_map(body, mesh=mesh, in_specs=in_specs, out_specs=out_specs, check_vma=False)
```

```python
import functools
import math

import jax
import jax.numpy as jnp
from jax import lax
from jax.experimental import pallas as pl
from jax.experimental.pallas import tpu as pltpu
from jax.sharding import PartitionSpec as P

DH = 128
TOK = 32
FEAT = 384
HC = 256
WIDTH = 3072
OUTC = 48
NZ, NYH, NX, NYL = 8, 2, 4, 4
NB = NYH * NX
F32 = jnp.float32
BF16 = jnp.bfloat16
MESH = pl.DeviceIdType.MESH


def dot_nt(a, b):
    return lax.dot_general(a, b, (((1,), (1,)), ((), ())), preferred_element_type=F32)


def dot_nn(a, b):
    return jnp.dot(a, b, preferred_element_type=F32)


def kernel(
    x_ref, stale_ref, w_ref, wo_ref, mod_ref, ids_ref, cos_ref, sin_ref, out_ref,
    ids_v, mod_v, w_v, xg, mg, a_v, kvs, kvf, kv1, qb, os_, orc, st, stc,
    wo, e0s, e0r, e1s, e1r, acc,
    in_sem, w_sem, xs_sem, xr_sem, ms_sem, mr_sem,
    ss_sem, sr_sem, fs_sem, fr_sem, qs_sem, qr_sem, os_sem, or_sem, ts_sem, tr_sem,
    wys_sem, wyr_sem, wzs_sem, wzr_sem, wxs_sem, wxr_sem,
    e0s_sem, e0r_sem, e1s_sem, e1r_sem,
):
    p = lax.axis_index("patch")
    h = lax.axis_index("head")
    z, b = p // NB, p % NB
    yh, x = b // NX, b % NX
    yl, c = h // 2, h % 2

    def z_peer(d):
        return (((z + d) % NZ) * NB + b, h)

    def x_peer(d):
        return (z * NB + yh * NX + (x + d) % NX, h)

    yh_peer = (z * NB + (1 - yh) * NX + x, h)
    sibling = (p, yl * 2 + 1 - c)

    def y_peer(d):
        return (p, ((yl + d) % NYL) * 2 + c)

    peers = [sibling, yh_peer]
    peers += [y_peer(d) for d in range(1, NYL)]
    peers += [x_peer(d) for d in range(1, NX)]
    peers += [z_peer(d) for d in range(1, NZ)]

    barrier = pltpu.get_barrier_semaphore()
    for peer in peers:
        pl.semaphore_signal(barrier, inc=1, device_id=peer, device_id_type=MESH)

    sent = []

    def send(src, dst, ssem, rsem, peer):
        copy = pltpu.make_async_remote_copy(
            src_ref=src, dst_ref=dst, send_sem=ssem, recv_sem=rsem, device_id=peer, device_id_type=MESH
        )
        copy.start()
        sent.append(copy)

    def arrived(dst, ssem, rsem, peer):
        pltpu.make_async_remote_copy(
            src_ref=dst, dst_ref=dst, send_sem=ssem, recv_sem=rsem, device_id=peer, device_id_type=MESH
        ).wait_recv()

    small = [
        pltpu.make_async_copy(ids_ref, ids_v, in_sem.at[0]),
        pltpu.make_async_copy(mod_ref, mod_v, in_sem.at[1]),
        pltpu.make_async_copy(x_ref, xg.at[h], in_sem.at[2]),
        pltpu.make_async_copy(stale_ref, kvs.at[0], in_sem.at[3]),
        pltpu.make_async_copy(wo_ref, wo.at[z, yh, x], in_sem.at[4]),
    ]
    for load in small:
        load.start()
    loads = [pltpu.make_async_copy(w_ref.at[t], w_v.at[t], w_sem.at[t]) for t in range(3)]
    for t in (1, 2, 0):
        loads[t].start()
    small[0].wait()
    small[1].wait()

    table_row = lax.broadcasted_iota(jnp.int32, (4, FEAT), 0)
    gates = []
    for s in range(2):
        pick = table_row == ids_v[s]
        rows = [jnp.sum(jnp.where(pick, mod_v[k], 0.0), axis=0, keepdims=True) for k in range(3)]
        mg[h, s : s + 1] = rows[0]
        mg[h, 2 + s : 3 + s] = rows[1]
        gates.append(rows[2])
    for load in small[2:]:
        load.wait()

    pl.semaphore_wait(barrier, len(peers))

    for s in range(2):
        for d in (2, 1, 3):
            send(xg.at[h, s], xg.at[h, s], xs_sem.at[s, d], xr_sem.at[s, h], y_peer(d))
            if s == 0:
                send(mg.at[h], mg.at[h], ms_sem.at[d], mr_sem.at[h], y_peer(d))
        send(xg.at[h, s], xg.at[h, s], xs_sem.at[s, 0], xr_sem.at[s, h], sibling)
        if s == 0:
            send(mg.at[h], mg.at[h], ms_sem.at[0], mr_sem.at[h], sibling)
    for d in range(1, NX):
        send(kvs.at[0], kvs.at[NX - d], ss_sem.at[d], sr_sem.at[NX - d], x_peer(d))
    send(kvs.at[0], kvs.at[NX], ss_sem.at[0], sr_sem.at[NX], yh_peer)
    send(wo.at[z, yh, x], wo.at[z, yh, x], wys_sem, wyr_sem, yh_peer)

    def rows_forward(s):
        for d in (1, 3, 2):
            hs = ((yl + d) % NYL) * 2 + c
            arrived(xg.at[hs, s], xs_sem.at[s, d], xr_sem.at[s, hs], y_peer(d))
            send(xg.at[hs, s], xg.at[hs, s], xs_sem.at[s, NYL - 1 + d], xr_sem.at[s, hs], sibling)
            if s == 0:
                arrived(mg.at[hs], ms_sem.at[d], mr_sem.at[hs], y_peer(d))
                send(mg.at[hs], mg.at[hs], ms_sem.at[NYL - 1 + d], mr_sem.at[hs], sibling)

    def rows_done(s):
        for d in range(NYL):
            hs = ((yl + d) % NYL) * 2 + 1 - c
            arrived(xg.at[hs, s], xs_sem.at[s, 0], xr_sem.at[s, hs], sibling)
            if s == 0:
                arrived(mg.at[hs], ms_sem.at[0], mr_sem.at[hs], sibling)

    def normalize(s):
        sum1 = jnp.zeros((TOK, 128), F32)
        sum2 = jnp.zeros((TOK, 128), F32)
        for j in range(8):
            v = xg[j, s].astype(F32)
            for k in range(FEAT // 128):
                part = v[:, k * 128 : (k + 1) * 128]
                sum1 += part
                sum2 += part * part
        mean = jnp.sum(sum1, axis=1, keepdims=True) / WIDTH
        square = jnp.sum(sum2, axis=1, keepdims=True) / WIDTH
        inv = lax.rsqrt(square - mean * mean + 1e-06)
        for j in range(8):
            v = (xg[j, s].astype(F32) - mean) * inv
            v = v * (1.0 + mg[j, 2 + s : 3 + s]) + mg[j, s : s + 1]
            a_v[s, :, j * FEAT : (j + 1) * FEAT] = v.astype(BF16)

    cos = cos_ref[...]
    sin = sin_ref[...]

    def rot(u):
        heads = []
        for i in range(2):
            uh = u[:, i * DH : (i + 1) * DH]
            heads.append(uh * cos + pltpu.roll(uh, DH // 2, 1) * sin)
        return jnp.concatenate(heads, axis=1).astype(BF16)

    def project_in(s, own):
        if s == 0:
            loads[1].wait()
        own[0] = rot(dot_nn(a_v[s], w_v[1]))
        if s == 0:
            loads[2].wait()
        own[1] = dot_nn(a_v[s], w_v[2]).astype(BF16)

    def queries(s):
        if s == 0:
            loads[0].wait()
        qb[0, s] = rot(dot_nn(a_v[s], w_v[0]))
        for d in (4, 3, 5, 2, 6, 1, 7):
            send(qb.at[0, s], qb.at[NZ - d, s], qs_sem.at[s, d], qr_sem.at[s, NZ - d], z_peer(d))

    def forward_wo(d):
        zz = (z + d) % NZ
        if d:
            arrived(wo.at[zz, :, x], wzs_sem.at[d], wzr_sem.at[zz], z_peer(d))
        for e in (2, 1, 3):
            send(wo.at[zz, :, x], wo.at[zz, :, x], wxs_sem.at[d, e], wxr_sem.at[x, zz], x_peer(e))

    rows_forward(0)
    rows_done(0)
    normalize(0)
    project_in(0, kvf.at[0])
    send(kvf.at[0], kvf.at[NX], fs_sem.at[0], fr_sem.at[NX], yh_peer)
    for d in range(1, NX):
        send(kvf.at[0], kvf.at[NX - d], fs_sem.at[d], fr_sem.at[NX - d], x_peer(d))
    rows_forward(1)
    queries(0)

    arrived(kvs.at[NX], ss_sem.at[0], sr_sem.at[NX], yh_peer)
    for d in range(1, NX):
        send(kvs.at[NX], kvs.at[NX + NX - d], ss_sem.at[NX + d], sr_sem.at[NX + NX - d], x_peer(d))
    arrived(wo.at[z, 1 - yh, x], wys_sem, wyr_sem, yh_peer)
    for d in (1, 7, 2, 6, 3, 5, 4):
        send(wo.at[z, :, x], wo.at[z, :, x], wzs_sem.at[d], wzr_sem.at[z], z_peer(d))
    forward_wo(0)

    rows_done(1)
    normalize(1)
    queries(1)
    project_in(1, kv1)

    for d in (1, 7):
        forward_wo(d)
    arrived(kvf.at[NX], fs_sem.at[0], fr_sem.at[NX], yh_peer)
    for d in range(1, NX):
        send(kvf.at[NX], kvf.at[NX + NX - d], fs_sem.at[NX + d], fr_sem.at[NX + NX - d], x_peer(d))
    for d in (2, 6):
        forward_wo(d)

    inv_root = 1.0 / math.sqrt(DH)
    ones = jnp.ones((NB * TOK, DH), BF16)
    diagonal = lax.broadcasted_iota(jnp.int32, (128, 128), 0) == lax.broadcasted_iota(jnp.int32, (128, 128), 1)

    def attend(s, held, own):
        for i in range(2):
            cols = slice(i * DH, (i + 1) * DH)
            keys = held[:, 0, :, cols].reshape(NB * TOK, DH)
            vals = held[:, 1, :, cols].reshape(NB * TOK, DH)
            own_keys = jnp.concatenate([own[0, :, cols], keys[TOK:]], axis=0)
            own_vals = jnp.concatenate([own[1, :, cols], vals[TOK:]], axis=0)
            q = qb[:, s, :, cols].reshape(NZ * TOK, DH)
            scores = jnp.concatenate([dot_nt(q[:TOK], own_keys), dot_nt(q[TOK:], keys)], axis=0) * inv_root
            top = jnp.max(scores, axis=1, keepdims=True)
            weights = jnp.exp(scores - top).astype(BF16)
            mixed = jnp.concatenate(
                [
                    dot_nn(weights[:TOK], jnp.concatenate([own_vals, ones], axis=1)),
                    dot_nn(weights[TOK:], jnp.concatenate([vals, ones], axis=1)),
                ],
                axis=0,
            )
            total = mixed[:, DH:]
            os_[s, :, :, cols] = (mixed[:, :DH] / total).astype(BF16).reshape(NZ, TOK, DH)
            lse = top + jnp.log(total)
            for k in range(NZ * TOK // 128):
                part = lse[k * 128 : (k + 1) * 128]
                row = jnp.sum(jnp.where(diagonal, part, 0.0), axis=0, keepdims=True)
                st[s, i : i + 1, k * 128 : (k + 1) * 128] = row
        for d in (4, 3, 5, 2, 6, 1, 7):
            send(os_.at[s, d], orc.at[s, NZ - d], os_sem.at[s, d], or_sem.at[s, NZ - d], z_peer(d))
            send(st.at[s], stc.at[s, NZ - d], ts_sem.at[s, d], tr_sem.at[s, NZ - d], z_peer(d))

    for d in range(1, NX):
        arrived(kvs.at[d], ss_sem.at[d], sr_sem.at[d], x_peer(d))
        arrived(kvs.at[NX + d], ss_sem.at[NX + d], sr_sem.at[NX + d], x_peer(d))
    for d in range(1, NZ):
        arrived(qb.at[d, 0], qs_sem.at[0, d], qr_sem.at[0, d], z_peer(d))
    attend(0, kvs, kvf.at[0])

    for d in (3, 5, 4):
        forward_wo(d)

    for d in range(1, NX):
        arrived(kvf.at[d], fs_sem.at[d], fr_sem.at[d], x_peer(d))
        arrived(kvf.at[NX + d], fs_sem.at[NX + d], fr_sem.at[NX + d], x_peer(d))
    for d in range(1, NZ):
        arrived(qb.at[d, 1], qs_sem.at[1, d], qr_sem.at[1, d], z_peer(d))
    attend(1, kvf, kv1)

    row_id = lax.broadcasted_iota(jnp.int32, (TOK, 128), 0)
    lane_id = lax.broadcasted_iota(jnp.int32, (TOK, 128), 1)

    def merge(s):
        for d in range(1, NZ):
            arrived(orc.at[s, d], os_sem.at[s, d], or_sem.at[s, d], z_peer(d))
            arrived(stc.at[s, d], ts_sem.at[s, d], tr_sem.at[s, d], z_peer(d))
        heads = []
        for i in range(2):
            lse = []
            for d in range(NZ):
                held = st if d == 0 else stc.at[:, d]
                at = (NZ - d) % NZ * TOK
                row = held[s, i : i + 1, at // 128 * 128 : at // 128 * 128 + 128]
                lse.append(jnp.sum(jnp.where(lane_id == row_id + at % 128, row, 0.0), axis=1, keepdims=True))
            top = functools.reduce(jnp.maximum, lse)
            mixed = jnp.zeros((TOK, DH), F32)
            total = jnp.zeros((TOK, 1), F32)
            for d in range(NZ):
                weight = jnp.exp(lse[d] - top)
                total += weight
                part = (os_ if d == 0 else orc)[s, d, :, i * DH : (i + 1) * DH]
                mixed += weight * part.astype(F32)
            heads.append((mixed / total).astype(BF16))
        return jnp.concatenate(heads, axis=1)

    def block(o, j, core):
        return dot_nt(o, wo[((yl + j) % NYL) * 2 + core].reshape(FEAT, HC))

    def project(s):
        o = merge(s)
        if s == 0:
            for e in range(1, NX):
                for zz in range(NZ):
                    xs = (x + e) % NX
                    arrived(wo.at[zz, :, xs], wxs_sem.at[0, e], wxr_sem.at[xs, zz], x_peer(e))
        for j in (2, 1, 3, 0):
            e0s[s, j] = block(o, j, 1 - c).astype(BF16)
            send(e0s.at[s, j], e0r.at[s, j], e0s_sem.at[s, j], e0r_sem.at[s, j], sibling)
        for j in (2, 1, 3, 0):
            mine = block(o, j, c)
            arrived(e0r.at[s, j], e0s_sem.at[s, j], e0r_sem.at[s, j], sibling)
            mine = mine + e0r[s, j].astype(F32)
            if j:
                e1s[s, j] = mine.astype(BF16)
                send(e1s.at[s, j], e1r.at[s, NYL - j], e1s_sem.at[s, j], e1r_sem.at[s, NYL - j], y_peer(j))
            else:
                acc[s] = mine

    project(0)
    project(1)
    for s in range(2):
        total = acc[s]
        for j in range(1, NYL):
            arrived(e1r.at[s, j], e1s_sem.at[s, j], e1r_sem.at[s, j], y_peer(j))
            total = total + e1r[s, j].astype(F32)
        out_ref[s * TOK : (s + 1) * TOK] = (gates[s] * total).astype(BF16)

    for copy in sent:
        copy.wait_send()


def tables(slab_order):
    positions = slab_order[0] * TOK + jnp.arange(TOK, dtype=jnp.int32)
    half = DH // 2
    frequency = 10000.0 ** (-(2.0 * jnp.arange(half, dtype=F32)) / DH)
    angle = positions.astype(F32)[:, None] * frequency[None, :]
    cos, sin = jnp.cos(angle), jnp.sin(angle)
    return jnp.concatenate([cos, cos], axis=1), jnp.concatenate([-sin, sin], axis=1)


def body(inputs, stale_kv, w_qkv, w_out, mod_table, step_ids, slab_order):
    cos, sin = tables(slab_order)
    vmem = pl.BlockSpec(memory_space=pltpu.VMEM)
    dma = pltpu.SemaphoreType.DMA
    out = pl.pallas_call(
        kernel,
        out_shape=jax.ShapeDtypeStruct((2 * TOK, FEAT), BF16),
        in_specs=[pl.BlockSpec(memory_space=pltpu.HBM)] * 6 + [vmem] * 2,
        out_specs=vmem,
        scratch_shapes=[
            pltpu.SMEM((2,), jnp.int32),
            pltpu.VMEM((3, 4, FEAT), F32),
            pltpu.VMEM((3, WIDTH, HC), BF16),
            pltpu.VMEM((8, 2, TOK, FEAT), BF16),
            pltpu.VMEM((8, 4, FEAT), F32),
            pltpu.VMEM((2, TOK, WIDTH), BF16),
            pltpu.VMEM((NB, 2, TOK, HC), BF16),
            pltpu.VMEM((NB, 2, TOK, HC), BF16),
            pltpu.VMEM((2, TOK, HC), BF16),
            pltpu.VMEM((NZ, 2, TOK, HC), BF16),
            pltpu.VMEM((2, NZ, TOK, HC), BF16),
            pltpu.VMEM((2, NZ, TOK, HC), BF16),
            pltpu.VMEM((2, 2, NZ * TOK), F32),
            pltpu.VMEM((2, NZ, 2, NZ * TOK), F32),
            pltpu.VMEM((NZ, NYH, NX, OUTC, HC), BF16),
            pltpu.VMEM((2, NYL, TOK, FEAT), BF16),
            pltpu.VMEM((2, NYL, TOK, FEAT), BF16),
            pltpu.VMEM((2, NYL, TOK, FEAT), BF16),
            pltpu.VMEM((2, NYL, TOK, FEAT), BF16),
            pltpu.VMEM((2, TOK, FEAT), F32),
            dma((5,)), dma((3,)),
            dma((2, 7)), dma((2, 8)), dma((7,)), dma((8,)),
            dma((8,)), dma((8,)), dma((8,)), dma((8,)),
            dma((2, 8)), dma((2, 8)), dma((2, 8)), dma((2, 8)), dma((2, 8)), dma((2, 8)),
            dma, dma, dma((8,)), dma((8,)), dma((8, 4)), dma((4, 8)),
            dma((2, 4)), dma((2, 4)), dma((2, 4)), dma((2, 4)),
        ],
        compiler_params=pltpu.CompilerParams(
            collective_id=0, has_side_effects=True, vmem_limit_bytes=60 * 1024 * 1024
        ),
        name="block",
    )(
        inputs,
        stale_kv,
        jnp.transpose(w_qkv, (1, 0, 2)),
        jnp.transpose(w_out),
        jnp.transpose(mod_table, (1, 0, 2)),
        step_ids,
        cos,
        sin,
    )
    return out.reshape(2, TOK, FEAT)


def solution(mesh):
    in_specs = (
        P(None, "patch", "head"),
        P(None, "patch", "head"),
        P(None, None, "head"),
        P("head", "patch"),
        P(None, None, "head"),
        P(),
        P("patch"),
    )
    out_specs = P(None, "patch", "head")
    return jax.shard_map(body, mesh=mesh, in_specs=in_specs, out_specs=out_specs, check_vma=False)
```

```python
import functools
import math

import jax
import jax.numpy as jnp
from jax import lax
from jax.experimental import pallas as pl
from jax.experimental.pallas import tpu as pltpu
from jax.sharding import PartitionSpec as P

DH = 128
TOK = 32
FEAT = 384
HC = 256
WIDTH = 3072
OUTC = 48
NZ, NYH, NX, NYL = 8, 2, 4, 4
NB = NYH * NX
RELAY = frozenset([(0, 0), (0, 1), (0, 2), (0, 3), (0, 4), (0, 5), (0, 6), (0, 7), (1, 0), (1, 1), (1, 2), (1, 3), (1, 4), (1, 5), (1, 6), (1, 7)])
F32 = jnp.float32
BF16 = jnp.bfloat16
MESH = pl.DeviceIdType.MESH


def dot_nt(a, b):
    return lax.dot_general(a, b, (((1,), (1,)), ((), ())), preferred_element_type=F32)


def dot_nn(a, b):
    return jnp.dot(a, b, preferred_element_type=F32)


def kernel(
    x_ref, stale_ref, w_ref, wo_ref, mod_ref, ids_ref, cos_ref, sin_ref, out_ref,
    ids_v, mod_v, w_v, xg, mg, a_v, kvs, kvf, kv1, qb, os_, orc, st, stc,
    wo, e0s, e0r, e1s, e1r, acc,
    in_sem, w_sem, xs_sem, xr_sem, ms_sem, mr_sem,
    ss_sem, sr_sem, fs_sem, fr_sem, qs_sem, qr_sem, os_sem, or_sem, ts_sem, tr_sem,
    wys_sem, wyr_sem, wzs_sem, wzr_sem, wxs_sem, wxr_sem,
    e0s_sem, e0r_sem, e1s_sem, e1r_sem,
):
    p = lax.axis_index("patch")
    h = lax.axis_index("head")
    z, b = p // NB, p % NB
    yh, x = b // NX, b % NX
    yl, c = h // 2, h % 2

    def z_peer(d):
        return (((z + d) % NZ) * NB + b, h)

    def x_peer(d):
        return (z * NB + yh * NX + (x + d) % NX, h)

    yh_peer = (z * NB + (1 - yh) * NX + x, h)
    sibling = (p, yl * 2 + 1 - c)

    def y_peer(d):
        return (p, ((yl + d) % NYL) * 2 + c)

    peers = [sibling, yh_peer]
    peers += [y_peer(d) for d in range(1, NYL)]
    peers += [x_peer(d) for d in range(1, NX)]
    peers += [z_peer(d) for d in range(1, NZ)]

    barrier = pltpu.get_barrier_semaphore()
    for peer in peers:
        pl.semaphore_signal(barrier, inc=1, device_id=peer, device_id_type=MESH)

    sent = []

    def send(src, dst, ssem, rsem, peer):
        copy = pltpu.make_async_remote_copy(
            src_ref=src, dst_ref=dst, send_sem=ssem, recv_sem=rsem, device_id=peer, device_id_type=MESH
        )
        copy.start()
        sent.append(copy)

    def arrived(dst, ssem, rsem, peer):
        pltpu.make_async_remote_copy(
            src_ref=dst, dst_ref=dst, send_sem=ssem, recv_sem=rsem, device_id=peer, device_id_type=MESH
        ).wait_recv()

    small = [
        pltpu.make_async_copy(ids_ref, ids_v, in_sem.at[0]),
        pltpu.make_async_copy(mod_ref, mod_v, in_sem.at[1]),
        pltpu.make_async_copy(x_ref, xg.at[h], in_sem.at[2]),
        pltpu.make_async_copy(stale_ref, kvs.at[0], in_sem.at[3]),
        pltpu.make_async_copy(wo_ref, wo.at[z, yh, x], in_sem.at[4]),
    ]
    for load in small:
        load.start()
    loads = [pltpu.make_async_copy(w_ref.at[t], w_v.at[t], w_sem.at[t]) for t in range(3)]
    for t in (1, 2, 0):
        loads[t].start()
    small[0].wait()
    small[1].wait()

    table_row = lax.broadcasted_iota(jnp.int32, (4, FEAT), 0)
    gates = []
    for s in range(2):
        pick = table_row == ids_v[s]
        rows = [jnp.sum(jnp.where(pick, mod_v[k], 0.0), axis=0, keepdims=True) for k in range(3)]
        mg[h, s : s + 1] = rows[0]
        mg[h, 2 + s : 3 + s] = rows[1]
        gates.append(rows[2])
    for load in small[2:]:
        load.wait()

    pl.semaphore_wait(barrier, len(peers))

    def wo_block(plane, dz, dx=0):
        return wo.at[(z + dz) % NZ, yh if plane == 0 else 1 - yh, (x + dx) % NX]

    relayed = set()

    def wo_along_x(plane, d):
        piece = wo_block(plane, d)
        for e in (1, 3) if (plane, d) in RELAY else (2, 1, 3):
            send(piece, piece, wxs_sem.at[plane, d, e], wxr_sem.at[plane, (NX - e) % NX, d], x_peer(e))

    def wo_relay(plane, d):
        e = 3 if plane == 0 else 1
        piece = wo_block(plane, d, e)
        arrived(piece, wxs_sem.at[plane, d, e], wxr_sem.at[plane, e, d], x_peer(e))
        send(piece, piece, wxs_sem.at[plane, d, 2], wxr_sem.at[plane, 2, d], x_peer(NX - e))
        relayed.add((plane, d, e))

    def wo_start(plane):
        piece = wo_block(plane, 0)
        for d in (1, 7, 2, 6, 3, 5, 4):
            send(piece, piece, wzs_sem.at[plane, d], wzr_sem.at[plane, NZ - d], z_peer(d))
        wo_along_x(plane, 0)

    def wo_forward(plane, d):
        arrived(wo_block(plane, d), wzs_sem.at[plane, d], wzr_sem.at[plane, d], z_peer(d))
        wo_along_x(plane, d)

    send(wo_block(0, 0), wo_block(0, 0), wys_sem, wyr_sem, yh_peer)
    for s in range(2):
        for d in (2, 1, 3):
            send(xg.at[h, s], xg.at[h, s], xs_sem.at[s, d], xr_sem.at[s, h], y_peer(d))
            if s == 0:
                send(mg.at[h], mg.at[h], ms_sem.at[d], mr_sem.at[h], y_peer(d))
        send(xg.at[h, s], xg.at[h, s], xs_sem.at[s, 0], xr_sem.at[s, h], sibling)
        if s == 0:
            send(mg.at[h], mg.at[h], ms_sem.at[0], mr_sem.at[h], sibling)
    wo_start(0)
    for d in range(1, NX):
        send(kvs.at[0], kvs.at[NX - d], ss_sem.at[d], sr_sem.at[NX - d], x_peer(d))
    send(kvs.at[0], kvs.at[NX], ss_sem.at[0], sr_sem.at[NX], yh_peer)

    def rows_forward(s):
        for d in (1, 3, 2):
            hs = ((yl + d) % NYL) * 2 + c
            arrived(xg.at[hs, s], xs_sem.at[s, d], xr_sem.at[s, hs], y_peer(d))
            send(xg.at[hs, s], xg.at[hs, s], xs_sem.at[s, NYL - 1 + d], xr_sem.at[s, hs], sibling)
            if s == 0:
                arrived(mg.at[hs], ms_sem.at[d], mr_sem.at[hs], y_peer(d))
                send(mg.at[hs], mg.at[hs], ms_sem.at[NYL - 1 + d], mr_sem.at[hs], sibling)

    def rows_done(s):
        for d in range(NYL):
            hs = ((yl + d) % NYL) * 2 + 1 - c
            arrived(xg.at[hs, s], xs_sem.at[s, 0], xr_sem.at[s, hs], sibling)
            if s == 0:
                arrived(mg.at[hs], ms_sem.at[0], mr_sem.at[hs], sibling)

    def normalize(s):
        sum1 = jnp.zeros((TOK, 128), F32)
        sum2 = jnp.zeros((TOK, 128), F32)
        for j in range(8):
            v = xg[j, s].astype(F32)
            for k in range(FEAT // 128):
                part = v[:, k * 128 : (k + 1) * 128]
                sum1 += part
                sum2 += part * part
        mean = jnp.sum(sum1, axis=1, keepdims=True) / WIDTH
        square = jnp.sum(sum2, axis=1, keepdims=True) / WIDTH
        inv = lax.rsqrt(square - mean * mean + 1e-06)
        for j in range(8):
            v = (xg[j, s].astype(F32) - mean) * inv
            v = v * (1.0 + mg[j, 2 + s : 3 + s]) + mg[j, s : s + 1]
            a_v[s, :, j * FEAT : (j + 1) * FEAT] = v.astype(BF16)

    cos = cos_ref[...]
    sin = sin_ref[...]

    def rot(u):
        heads = []
        for i in range(2):
            uh = u[:, i * DH : (i + 1) * DH]
            heads.append(uh * cos + pltpu.roll(uh, DH // 2, 1) * sin)
        return jnp.concatenate(heads, axis=1).astype(BF16)

    def project_in(s, own):
        if s == 0:
            loads[1].wait()
        own[0] = rot(dot_nn(a_v[s], w_v[1]))
        if s == 0:
            loads[2].wait()
        own[1] = dot_nn(a_v[s], w_v[2]).astype(BF16)

    def queries(s):
        if s == 0:
            loads[0].wait()
        qb[0, s] = rot(dot_nn(a_v[s], w_v[0]))
        for d in (4, 3, 5, 2, 6, 1, 7):
            send(qb.at[0, s], qb.at[NZ - d, s], qs_sem.at[s, d], qr_sem.at[s, NZ - d], z_peer(d))

    rows_forward(0)
    arrived(wo_block(1, 0), wys_sem, wyr_sem, yh_peer)
    wo_start(1)
    rows_done(0)
    normalize(0)
    project_in(0, kvf.at[0])
    send(kvf.at[0], kvf.at[NX], fs_sem.at[0], fr_sem.at[NX], yh_peer)
    for d in range(1, NX):
        send(kvf.at[0], kvf.at[NX - d], fs_sem.at[d], fr_sem.at[NX - d], x_peer(d))
    rows_forward(1)
    queries(0)

    arrived(kvs.at[NX], ss_sem.at[0], sr_sem.at[NX], yh_peer)
    for d in range(1, NX):
        send(kvs.at[NX], kvs.at[NX + NX - d], ss_sem.at[NX + d], sr_sem.at[NX + NX - d], x_peer(d))
    for d in (1, 7, 2, 6):
        wo_forward(0, d)

    rows_done(1)
    normalize(1)
    queries(1)
    project_in(1, kv1)
    for d in (0,):
        wo_relay(0, d)

    for d in (3, 5, 4):
        wo_forward(0, d)
    arrived(kvf.at[NX], fs_sem.at[0], fr_sem.at[NX], yh_peer)
    for d in range(1, NX):
        send(kvf.at[NX], kvf.at[NX + NX - d], fs_sem.at[NX + d], fr_sem.at[NX + NX - d], x_peer(d))
    for d in (1, 7, 2, 6):
        wo_forward(1, d)
    for d in (1, 7, 2, 6,):
        wo_relay(0, d)
    for d in (0,):
        wo_relay(1, d)

    inv_root = 1.0 / math.sqrt(DH)
    ones = jnp.ones((NB * TOK, DH), BF16)
    diagonal = lax.broadcasted_iota(jnp.int32, (128, 128), 0) == lax.broadcasted_iota(jnp.int32, (128, 128), 1)

    def attend(s, held, own):
        for i in range(2):
            cols = slice(i * DH, (i + 1) * DH)
            keys = held[:, 0, :, cols].reshape(NB * TOK, DH)
            vals = held[:, 1, :, cols].reshape(NB * TOK, DH)
            own_keys = jnp.concatenate([own[0, :, cols], keys[TOK:]], axis=0)
            own_vals = jnp.concatenate([own[1, :, cols], vals[TOK:]], axis=0)
            q = qb[:, s, :, cols].reshape(NZ * TOK, DH)
            scores = jnp.concatenate([dot_nt(q[:TOK], own_keys), dot_nt(q[TOK:], keys)], axis=0) * inv_root
            top = jnp.max(scores, axis=1, keepdims=True)
            weights = jnp.exp(scores - top).astype(BF16)
            mixed = jnp.concatenate(
                [
                    dot_nn(weights[:TOK], jnp.concatenate([own_vals, ones], axis=1)),
                    dot_nn(weights[TOK:], jnp.concatenate([vals, ones], axis=1)),
                ],
                axis=0,
            )
            total = mixed[:, DH:]
            os_[s, :, :, cols] = (mixed[:, :DH] / total).astype(BF16).reshape(NZ, TOK, DH)
            lse = top + jnp.log(total)
            for k in range(NZ * TOK // 128):
                part = lse[k * 128 : (k + 1) * 128]
                row = jnp.sum(jnp.where(diagonal, part, 0.0), axis=0, keepdims=True)
                st[s, i : i + 1, k * 128 : (k + 1) * 128] = row
        for d in (4, 3, 5, 2, 6, 1, 7):
            send(os_.at[s, d], orc.at[s, NZ - d], os_sem.at[s, d], or_sem.at[s, NZ - d], z_peer(d))
            send(st.at[s], stc.at[s, NZ - d], ts_sem.at[s, d], tr_sem.at[s, NZ - d], z_peer(d))

    for d in range(1, NX):
        arrived(kvs.at[d], ss_sem.at[d], sr_sem.at[d], x_peer(d))
        arrived(kvs.at[NX + d], ss_sem.at[NX + d], sr_sem.at[NX + d], x_peer(d))
    for d in range(1, NZ):
        arrived(qb.at[d, 0], qs_sem.at[0, d], qr_sem.at[0, d], z_peer(d))
    attend(0, kvs, kvf.at[0])
    for d in (3, 5, 4):
        wo_forward(1, d)
    for d in (3, 5, 4,):
        wo_relay(0, d)


    for d in range(1, NX):
        arrived(kvf.at[d], fs_sem.at[d], fr_sem.at[d], x_peer(d))
        arrived(kvf.at[NX + d], fs_sem.at[NX + d], fr_sem.at[NX + d], x_peer(d))
    for d in range(1, NZ):
        arrived(qb.at[d, 1], qs_sem.at[1, d], qr_sem.at[1, d], z_peer(d))
    attend(1, kvf, kv1)
    for d in (1, 7, 2, 6, 3, 5, 4,):
        wo_relay(1, d)

    row_id = lax.broadcasted_iota(jnp.int32, (TOK, 128), 0)
    lane_id = lax.broadcasted_iota(jnp.int32, (TOK, 128), 1)

    def merge(s):
        for d in range(1, NZ):
            arrived(orc.at[s, d], os_sem.at[s, d], or_sem.at[s, d], z_peer(d))
            arrived(stc.at[s, d], ts_sem.at[s, d], tr_sem.at[s, d], z_peer(d))
        heads = []
        for i in range(2):
            lse = []
            for d in range(NZ):
                held = st if d == 0 else stc.at[:, d]
                at = (NZ - d) % NZ * TOK
                row = held[s, i : i + 1, at // 128 * 128 : at // 128 * 128 + 128]
                lse.append(jnp.sum(jnp.where(lane_id == row_id + at % 128, row, 0.0), axis=1, keepdims=True))
            top = functools.reduce(jnp.maximum, lse)
            mixed = jnp.zeros((TOK, DH), F32)
            total = jnp.zeros((TOK, 1), F32)
            for d in range(NZ):
                weight = jnp.exp(lse[d] - top)
                total += weight
                part = (os_ if d == 0 else orc)[s, d, :, i * DH : (i + 1) * DH]
                mixed += weight * part.astype(F32)
            heads.append((mixed / total).astype(BF16))
        return jnp.concatenate(heads, axis=1)

    def block(o, j, core):
        return dot_nt(o, wo[((yl + j) % NYL) * 2 + core].reshape(FEAT, HC))

    def project(s):
        o = merge(s)
        if s == 0:
            for e in range(1, NX):
                for d in range(NZ):
                    for plane in range(NYH):
                        if (plane, d, e) in relayed:
                            continue
                        arrived(wo_block(plane, d, e), wxs_sem.at[plane, d, e], wxr_sem.at[plane, e, d], x_peer(e))
        for j in (2, 1, 3, 0):
            e0s[s, j] = block(o, j, 1 - c).astype(BF16)
            send(e0s.at[s, j], e0r.at[s, j], e0s_sem.at[s, j], e0r_sem.at[s, j], sibling)
        for j in (2, 1, 3, 0):
            mine = block(o, j, c)
            arrived(e0r.at[s, j], e0s_sem.at[s, j], e0r_sem.at[s, j], sibling)
            mine = mine + e0r[s, j].astype(F32)
            if j:
                e1s[s, j] = mine.astype(BF16)
                send(e1s.at[s, j], e1r.at[s, NYL - j], e1s_sem.at[s, j], e1r_sem.at[s, NYL - j], y_peer(j))
            else:
                acc[s] = mine

    project(0)
    project(1)
    for s in range(2):
        total = acc[s]
        for j in range(1, NYL):
            arrived(e1r.at[s, j], e1s_sem.at[s, j], e1r_sem.at[s, j], y_peer(j))
            total = total + e1r[s, j].astype(F32)
        out_ref[s * TOK : (s + 1) * TOK] = (gates[s] * total).astype(BF16)

    for copy in sent:
        copy.wait_send()


def tables(slab_order):
    positions = slab_order[0] * TOK + jnp.arange(TOK, dtype=jnp.int32)
    half = DH // 2
    frequency = 10000.0 ** (-(2.0 * jnp.arange(half, dtype=F32)) / DH)
    angle = positions.astype(F32)[:, None] * frequency[None, :]
    cos, sin = jnp.cos(angle), jnp.sin(angle)
    return jnp.concatenate([cos, cos], axis=1), jnp.concatenate([-sin, sin], axis=1)


def body(inputs, stale_kv, w_qkv, w_out, mod_table, step_ids, slab_order):
    cos, sin = tables(slab_order)
    vmem = pl.BlockSpec(memory_space=pltpu.VMEM)
    dma = pltpu.SemaphoreType.DMA
    out = pl.pallas_call(
        kernel,
        out_shape=jax.ShapeDtypeStruct((2 * TOK, FEAT), BF16),
        in_specs=[pl.BlockSpec(memory_space=pltpu.HBM)] * 6 + [vmem] * 2,
        out_specs=vmem,
        scratch_shapes=[
            pltpu.SMEM((2,), jnp.int32),
            pltpu.VMEM((3, 4, FEAT), F32),
            pltpu.VMEM((3, WIDTH, HC), BF16),
            pltpu.VMEM((8, 2, TOK, FEAT), BF16),
            pltpu.VMEM((8, 4, FEAT), F32),
            pltpu.VMEM((2, TOK, WIDTH), BF16),
            pltpu.VMEM((NB, 2, TOK, HC), BF16),
            pltpu.VMEM((NB, 2, TOK, HC), BF16),
            pltpu.VMEM((2, TOK, HC), BF16),
            pltpu.VMEM((NZ, 2, TOK, HC), BF16),
            pltpu.VMEM((2, NZ, TOK, HC), BF16),
            pltpu.VMEM((2, NZ, TOK, HC), BF16),
            pltpu.VMEM((2, 2, NZ * TOK), F32),
            pltpu.VMEM((2, NZ, 2, NZ * TOK), F32),
            pltpu.VMEM((NZ, NYH, NX, OUTC, HC), BF16),
            pltpu.VMEM((2, NYL, TOK, FEAT), BF16),
            pltpu.VMEM((2, NYL, TOK, FEAT), BF16),
            pltpu.VMEM((2, NYL, TOK, FEAT), BF16),
            pltpu.VMEM((2, NYL, TOK, FEAT), BF16),
            pltpu.VMEM((2, TOK, FEAT), F32),
            dma((5,)), dma((3,)),
            dma((2, 7)), dma((2, 8)), dma((7,)), dma((8,)),
            dma((8,)), dma((8,)), dma((8,)), dma((8,)),
            dma((2, 8)), dma((2, 8)), dma((2, 8)), dma((2, 8)), dma((2, 8)), dma((2, 8)),
            dma, dma, dma((2, 8)), dma((2, 8)), dma((2, 8, 4)), dma((2, 4, 8)),
            dma((2, 4)), dma((2, 4)), dma((2, 4)), dma((2, 4)),
        ],
        compiler_params=pltpu.CompilerParams(
            collective_id=0, has_side_effects=True, vmem_limit_bytes=60 * 1024 * 1024
        ),
        name="block",
    )(
        inputs,
        stale_kv,
        jnp.transpose(w_qkv, (1, 0, 2)),
        jnp.transpose(w_out),
        jnp.transpose(mod_table, (1, 0, 2)),
        step_ids,
        cos,
        sin,
    )
    return out.reshape(2, TOK, FEAT)


def solution(mesh):
    in_specs = (
        P(None, "patch", "head"),
        P(None, "patch", "head"),
        P(None, None, "head"),
        P("head", "patch"),
        P(None, None, "head"),
        P(),
        P("patch"),
    )
    out_specs = P(None, "patch", "head")
    return jax.shard_map(body, mesh=mesh, in_specs=in_specs, out_specs=out_specs, check_vma=False)
```

```python
import functools
import math

import jax
import jax.numpy as jnp
from jax import lax
from jax.experimental import pallas as pl
from jax.experimental.pallas import tpu as pltpu
from jax.sharding import PartitionSpec as P

DH = 128
TOK = 32
FEAT = 384
HC = 256
WIDTH = 3072
OUTC = 48
NZ, NYH, NX, NYL = 8, 2, 4, 4
NB = NYH * NX
RELAY = frozenset([(0, 0), (0, 1), (0, 2), (0, 3), (0, 4), (0, 5), (0, 6), (0, 7), (1, 0), (1, 1), (1, 2), (1, 3), (1, 4), (1, 5), (1, 6), (1, 7)])
F32 = jnp.float32
BF16 = jnp.bfloat16
MESH = pl.DeviceIdType.MESH


def dot_nt(a, b):
    return lax.dot_general(a, b, (((1,), (1,)), ((), ())), preferred_element_type=F32)


def dot_nn(a, b):
    return jnp.dot(a, b, preferred_element_type=F32)


def kernel(
    x_ref, stale_ref, w_ref, wo_ref, mod_ref, ids_ref, order_ref, out_ref,
    ids_v, order_v, mod_v, w_v, xg, mg, a_v, kvs, kvf, kv1, qb, os_, orc, st, stc,
    wo, e0s, e0r, e1s, e1r, acc,
    in_sem, w_sem, xs_sem, xr_sem, ms_sem, mr_sem,
    ss_sem, sr_sem, fs_sem, fr_sem, qs_sem, qr_sem, os_sem, or_sem, ts_sem, tr_sem,
    wys_sem, wyr_sem, wzs_sem, wzr_sem, wxs_sem, wxr_sem,
    e0s_sem, e0r_sem, e1s_sem, e1r_sem,
):
    p = lax.axis_index("patch")
    h = lax.axis_index("head")
    z, b = p // NB, p % NB
    yh, x = b // NX, b % NX
    yl, c = h // 2, h % 2

    def z_peer(d):
        return (((z + d) % NZ) * NB + b, h)

    def x_peer(d):
        return (z * NB + yh * NX + (x + d) % NX, h)

    yh_peer = (z * NB + (1 - yh) * NX + x, h)
    sibling = (p, yl * 2 + 1 - c)

    def y_peer(d):
        return (p, ((yl + d) % NYL) * 2 + c)

    peers = [sibling, yh_peer]
    peers += [y_peer(d) for d in range(1, NYL)]
    peers += [x_peer(d) for d in range(1, NX)]
    peers += [z_peer(d) for d in range(1, NZ)]

    barrier = pltpu.get_barrier_semaphore()
    for peer in peers:
        pl.semaphore_signal(barrier, inc=1, device_id=peer, device_id_type=MESH)

    sent = []

    def send(src, dst, ssem, rsem, peer):
        copy = pltpu.make_async_remote_copy(
            src_ref=src, dst_ref=dst, send_sem=ssem, recv_sem=rsem, device_id=peer, device_id_type=MESH
        )
        copy.start()
        sent.append(copy)

    def arrived(dst, ssem, rsem, peer):
        pltpu.make_async_remote_copy(
            src_ref=dst, dst_ref=dst, send_sem=ssem, recv_sem=rsem, device_id=peer, device_id_type=MESH
        ).wait_recv()

    small = [
        pltpu.make_async_copy(ids_ref, ids_v, in_sem.at[0]),
        pltpu.make_async_copy(order_ref, order_v, in_sem.at[5]),
        pltpu.make_async_copy(mod_ref, mod_v, in_sem.at[1]),
        pltpu.make_async_copy(x_ref, xg.at[h], in_sem.at[2]),
        pltpu.make_async_copy(stale_ref, kvs.at[0], in_sem.at[3]),
        pltpu.make_async_copy(wo_ref, wo.at[z, yh, x], in_sem.at[4]),
    ]
    for load in small:
        load.start()
    loads = [pltpu.make_async_copy(w_ref.at[t], w_v.at[t], w_sem.at[t]) for t in range(3)]
    for t in (1, 2, 0):
        loads[t].start()
    for load in small[:3]:
        load.wait()

    table_row = lax.broadcasted_iota(jnp.int32, (4, FEAT), 0)
    gates = []
    for s in range(2):
        pick = table_row == ids_v[s]
        rows = [jnp.sum(jnp.where(pick, mod_v[k], 0.0), axis=0, keepdims=True) for k in range(3)]
        mg[h, s : s + 1] = rows[0]
        mg[h, 2 + s : 3 + s] = rows[1]
        gates.append(rows[2])
    token = lax.broadcasted_iota(jnp.int32, (TOK, DH), 0)
    lane = lax.broadcasted_iota(jnp.int32, (TOK, DH), 1)
    half = DH // 2
    exponent = jnp.where(lane < half, lane, lane - half).astype(F32) * (-math.log(10000.0) / half)
    angle = (order_v[0] * TOK + token).astype(F32) * jnp.exp(exponent)
    cos = jnp.cos(angle)
    sin = jnp.where(lane < half, -1.0, 1.0) * jnp.sin(angle)
    for load in small[3:]:
        load.wait()

    pl.semaphore_wait(barrier, len(peers))

    def wo_block(plane, dz, dx=0):
        return wo.at[(z + dz) % NZ, yh if plane == 0 else 1 - yh, (x + dx) % NX]

    relayed = set()

    def wo_along_x(plane, d):
        piece = wo_block(plane, d)
        for e in (1, 3) if (plane, d) in RELAY else (2, 1, 3):
            send(piece, piece, wxs_sem.at[plane, d, e], wxr_sem.at[plane, (NX - e) % NX, d], x_peer(e))

    def wo_relay(plane, d):
        e = 3 if plane == 0 else 1
        piece = wo_block(plane, d, e)
        arrived(piece, wxs_sem.at[plane, d, e], wxr_sem.at[plane, e, d], x_peer(e))
        send(piece, piece, wxs_sem.at[plane, d, 2], wxr_sem.at[plane, 2, d], x_peer(NX - e))
        relayed.add((plane, d, e))

    def wo_start(plane):
        piece = wo_block(plane, 0)
        for d in (1, 7, 2, 6, 3, 5, 4):
            send(piece, piece, wzs_sem.at[plane, d], wzr_sem.at[plane, NZ - d], z_peer(d))
        wo_along_x(plane, 0)

    def wo_forward(plane, d):
        arrived(wo_block(plane, d), wzs_sem.at[plane, d], wzr_sem.at[plane, d], z_peer(d))
        wo_along_x(plane, d)

    send(wo_block(0, 0), wo_block(0, 0), wys_sem, wyr_sem, yh_peer)
    for s in range(2):
        for d in (2, 1, 3):
            send(xg.at[h, s], xg.at[h, s], xs_sem.at[s, d], xr_sem.at[s, h], y_peer(d))
            if s == 0:
                send(mg.at[h], mg.at[h], ms_sem.at[d], mr_sem.at[h], y_peer(d))
        send(xg.at[h, s], xg.at[h, s], xs_sem.at[s, 0], xr_sem.at[s, h], sibling)
        if s == 0:
            send(mg.at[h], mg.at[h], ms_sem.at[0], mr_sem.at[h], sibling)
    wo_start(0)
    for d in range(1, NX):
        send(kvs.at[0], kvs.at[NX - d], ss_sem.at[d], sr_sem.at[NX - d], x_peer(d))
    send(kvs.at[0], kvs.at[NX], ss_sem.at[0], sr_sem.at[NX], yh_peer)

    def rows_forward(s):
        for d in (1, 3, 2):
            hs = ((yl + d) % NYL) * 2 + c
            arrived(xg.at[hs, s], xs_sem.at[s, d], xr_sem.at[s, hs], y_peer(d))
            send(xg.at[hs, s], xg.at[hs, s], xs_sem.at[s, NYL - 1 + d], xr_sem.at[s, hs], sibling)
            if s == 0:
                arrived(mg.at[hs], ms_sem.at[d], mr_sem.at[hs], y_peer(d))
                send(mg.at[hs], mg.at[hs], ms_sem.at[NYL - 1 + d], mr_sem.at[hs], sibling)

    def rows_done(s):
        for d in range(NYL):
            hs = ((yl + d) % NYL) * 2 + 1 - c
            arrived(xg.at[hs, s], xs_sem.at[s, 0], xr_sem.at[s, hs], sibling)
            if s == 0:
                arrived(mg.at[hs], ms_sem.at[0], mr_sem.at[hs], sibling)

    def normalize(s):
        sum1 = jnp.zeros((TOK, 128), F32)
        sum2 = jnp.zeros((TOK, 128), F32)
        for j in range(8):
            v = xg[j, s].astype(F32)
            for k in range(FEAT // 128):
                part = v[:, k * 128 : (k + 1) * 128]
                sum1 += part
                sum2 += part * part
        mean = jnp.sum(sum1, axis=1, keepdims=True) / WIDTH
        square = jnp.sum(sum2, axis=1, keepdims=True) / WIDTH
        inv = lax.rsqrt(square - mean * mean + 1e-06)
        for j in range(8):
            v = (xg[j, s].astype(F32) - mean) * inv
            v = v * (1.0 + mg[j, 2 + s : 3 + s]) + mg[j, s : s + 1]
            a_v[s, :, j * FEAT : (j + 1) * FEAT] = v.astype(BF16)

    def rot(u):
        heads = []
        for i in range(2):
            uh = u[:, i * DH : (i + 1) * DH]
            heads.append(uh * cos + pltpu.roll(uh, DH // 2, 1) * sin)
        return jnp.concatenate(heads, axis=1).astype(BF16)

    def project_in(s, own):
        if s == 0:
            loads[1].wait()
        own[0] = rot(dot_nn(a_v[s], w_v[1]))
        if s == 0:
            loads[2].wait()
        own[1] = dot_nn(a_v[s], w_v[2]).astype(BF16)

    def queries(s):
        if s == 0:
            loads[0].wait()
        qb[0, s] = rot(dot_nn(a_v[s], w_v[0]))
        for d in (4, 3, 5, 2, 6, 1, 7):
            send(qb.at[0, s], qb.at[NZ - d, s], qs_sem.at[s, d], qr_sem.at[s, NZ - d], z_peer(d))

    rows_forward(0)
    arrived(wo_block(1, 0), wys_sem, wyr_sem, yh_peer)
    wo_start(1)
    rows_done(0)
    normalize(0)
    project_in(0, kvf.at[0])
    send(kvf.at[0], kvf.at[NX], fs_sem.at[0], fr_sem.at[NX], yh_peer)
    for d in range(1, NX):
        send(kvf.at[0], kvf.at[NX - d], fs_sem.at[d], fr_sem.at[NX - d], x_peer(d))
    rows_forward(1)
    queries(0)

    arrived(kvs.at[NX], ss_sem.at[0], sr_sem.at[NX], yh_peer)
    for d in range(1, NX):
        send(kvs.at[NX], kvs.at[NX + NX - d], ss_sem.at[NX + d], sr_sem.at[NX + NX - d], x_peer(d))
    for d in (1, 7, 2, 6):
        wo_forward(0, d)

    rows_done(1)
    normalize(1)
    queries(1)
    project_in(1, kv1)
    for d in (0,):
        wo_relay(0, d)

    for d in (3, 5, 4):
        wo_forward(0, d)
    arrived(kvf.at[NX], fs_sem.at[0], fr_sem.at[NX], yh_peer)
    for d in range(1, NX):
        send(kvf.at[NX], kvf.at[NX + NX - d], fs_sem.at[NX + d], fr_sem.at[NX + NX - d], x_peer(d))
    for d in (1, 7, 2, 6):
        wo_forward(1, d)
    for d in (1, 7, 2, 6,):
        wo_relay(0, d)
    for d in (0,):
        wo_relay(1, d)

    inv_root = 1.0 / math.sqrt(DH)
    ones = jnp.ones((NB * TOK, DH), BF16)
    diagonal = lax.broadcasted_iota(jnp.int32, (128, 128), 0) == lax.broadcasted_iota(jnp.int32, (128, 128), 1)

    def attend(s, held, own):
        for i in range(2):
            cols = slice(i * DH, (i + 1) * DH)
            keys = held[:, 0, :, cols].reshape(NB * TOK, DH)
            vals = held[:, 1, :, cols].reshape(NB * TOK, DH)
            own_keys = jnp.concatenate([own[0, :, cols], keys[TOK:]], axis=0)
            own_vals = jnp.concatenate([own[1, :, cols], vals[TOK:]], axis=0)
            q = qb[:, s, :, cols].reshape(NZ * TOK, DH)
            scores = jnp.concatenate([dot_nt(q[:TOK], own_keys), dot_nt(q[TOK:], keys)], axis=0) * inv_root
            top = jnp.max(scores, axis=1, keepdims=True)
            weights = jnp.exp(scores - top).astype(BF16)
            mixed = jnp.concatenate(
                [
                    dot_nn(weights[:TOK], jnp.concatenate([own_vals, ones], axis=1)),
                    dot_nn(weights[TOK:], jnp.concatenate([vals, ones], axis=1)),
                ],
                axis=0,
            )
            total = mixed[:, DH:]
            os_[s, :, :, cols] = (mixed[:, :DH] / total).astype(BF16).reshape(NZ, TOK, DH)
            lse = top + jnp.log(total)
            for k in range(NZ * TOK // 128):
                part = lse[k * 128 : (k + 1) * 128]
                row = jnp.sum(jnp.where(diagonal, part, 0.0), axis=0, keepdims=True)
                st[s, i : i + 1, k * 128 : (k + 1) * 128] = row
        for d in (4, 3, 5, 2, 6, 1, 7):
            send(os_.at[s, d], orc.at[s, NZ - d], os_sem.at[s, d], or_sem.at[s, NZ - d], z_peer(d))
            send(st.at[s], stc.at[s, NZ - d], ts_sem.at[s, d], tr_sem.at[s, NZ - d], z_peer(d))

    for d in range(1, NX):
        arrived(kvs.at[d], ss_sem.at[d], sr_sem.at[d], x_peer(d))
        arrived(kvs.at[NX + d], ss_sem.at[NX + d], sr_sem.at[NX + d], x_peer(d))
    for d in range(1, NZ):
        arrived(qb.at[d, 0], qs_sem.at[0, d], qr_sem.at[0, d], z_peer(d))
    attend(0, kvs, kvf.at[0])
    for d in (3, 5, 4):
        wo_forward(1, d)
    for d in (3, 5, 4,):
        wo_relay(0, d)


    for d in range(1, NX):
        arrived(kvf.at[d], fs_sem.at[d], fr_sem.at[d], x_peer(d))
        arrived(kvf.at[NX + d], fs_sem.at[NX + d], fr_sem.at[NX + d], x_peer(d))
    for d in range(1, NZ):
        arrived(qb.at[d, 1], qs_sem.at[1, d], qr_sem.at[1, d], z_peer(d))
    attend(1, kvf, kv1)
    for d in (1, 7, 2, 6, 3, 5, 4,):
        wo_relay(1, d)

    row_id = lax.broadcasted_iota(jnp.int32, (TOK, 128), 0)
    lane_id = lax.broadcasted_iota(jnp.int32, (TOK, 128), 1)

    def merge(s):
        for d in range(1, NZ):
            arrived(orc.at[s, d], os_sem.at[s, d], or_sem.at[s, d], z_peer(d))
            arrived(stc.at[s, d], ts_sem.at[s, d], tr_sem.at[s, d], z_peer(d))
        heads = []
        for i in range(2):
            lse = []
            for d in range(NZ):
                held = st if d == 0 else stc.at[:, d]
                at = (NZ - d) % NZ * TOK
                row = held[s, i : i + 1, at // 128 * 128 : at // 128 * 128 + 128]
                lse.append(jnp.sum(jnp.where(lane_id == row_id + at % 128, row, 0.0), axis=1, keepdims=True))
            top = functools.reduce(jnp.maximum, lse)
            mixed = jnp.zeros((TOK, DH), F32)
            total = jnp.zeros((TOK, 1), F32)
            for d in range(NZ):
                weight = jnp.exp(lse[d] - top)
                total += weight
                part = (os_ if d == 0 else orc)[s, d, :, i * DH : (i + 1) * DH]
                mixed += weight * part.astype(F32)
            heads.append((mixed / total).astype(BF16))
        return jnp.concatenate(heads, axis=1)

    def block(o, j, core):
        return dot_nt(o, wo[((yl + j) % NYL) * 2 + core].reshape(FEAT, HC))

    def project(s):
        o = merge(s)
        if s == 0:
            for e in range(1, NX):
                for d in range(NZ):
                    for plane in range(NYH):
                        if (plane, d, e) in relayed:
                            continue
                        arrived(wo_block(plane, d, e), wxs_sem.at[plane, d, e], wxr_sem.at[plane, e, d], x_peer(e))
        for j in (2, 1, 3, 0):
            e0s[s, j] = block(o, j, 1 - c).astype(BF16)
            send(e0s.at[s, j], e0r.at[s, j], e0s_sem.at[s, j], e0r_sem.at[s, j], sibling)
        for j in (2, 1, 3, 0):
            mine = block(o, j, c)
            arrived(e0r.at[s, j], e0s_sem.at[s, j], e0r_sem.at[s, j], sibling)
            mine = mine + e0r[s, j].astype(F32)
            if j:
                e1s[s, j] = mine.astype(BF16)
                send(e1s.at[s, j], e1r.at[s, NYL - j], e1s_sem.at[s, j], e1r_sem.at[s, NYL - j], y_peer(j))
            else:
                acc[s] = mine

    project(0)
    project(1)
    for s in range(2):
        total = acc[s]
        for j in range(1, NYL):
            arrived(e1r.at[s, j], e1s_sem.at[s, j], e1r_sem.at[s, j], y_peer(j))
            total = total + e1r[s, j].astype(F32)
        out_ref[s * TOK : (s + 1) * TOK] = (gates[s] * total).astype(BF16)

    for copy in sent:
        copy.wait_send()


def body(inputs, stale_kv, w_qkv, w_out, mod_table, step_ids, slab_order):
    vmem = pl.BlockSpec(memory_space=pltpu.VMEM)
    dma = pltpu.SemaphoreType.DMA
    out = pl.pallas_call(
        kernel,
        out_shape=jax.ShapeDtypeStruct((2 * TOK, FEAT), BF16),
        in_specs=[pl.BlockSpec(memory_space=pltpu.HBM)] * 7,
        out_specs=vmem,
        scratch_shapes=[
            pltpu.SMEM((2,), jnp.int32),
            pltpu.SMEM((1,), jnp.int32),
            pltpu.VMEM((3, 4, FEAT), F32),
            pltpu.VMEM((3, WIDTH, HC), BF16),
            pltpu.VMEM((8, 2, TOK, FEAT), BF16),
            pltpu.VMEM((8, 4, FEAT), F32),
            pltpu.VMEM((2, TOK, WIDTH), BF16),
            pltpu.VMEM((NB, 2, TOK, HC), BF16),
            pltpu.VMEM((NB, 2, TOK, HC), BF16),
            pltpu.VMEM((2, TOK, HC), BF16),
            pltpu.VMEM((NZ, 2, TOK, HC), BF16),
            pltpu.VMEM((2, NZ, TOK, HC), BF16),
            pltpu.VMEM((2, NZ, TOK, HC), BF16),
            pltpu.VMEM((2, 2, NZ * TOK), F32),
            pltpu.VMEM((2, NZ, 2, NZ * TOK), F32),
            pltpu.VMEM((NZ, NYH, NX, OUTC, HC), BF16),
            pltpu.VMEM((2, NYL, TOK, FEAT), BF16),
            pltpu.VMEM((2, NYL, TOK, FEAT), BF16),
            pltpu.VMEM((2, NYL, TOK, FEAT), BF16),
            pltpu.VMEM((2, NYL, TOK, FEAT), BF16),
            pltpu.VMEM((2, TOK, FEAT), F32),
            dma((6,)), dma((3,)),
            dma((2, 7)), dma((2, 8)), dma((7,)), dma((8,)),
            dma((8,)), dma((8,)), dma((8,)), dma((8,)),
            dma((2, 8)), dma((2, 8)), dma((2, 8)), dma((2, 8)), dma((2, 8)), dma((2, 8)),
            dma, dma, dma((2, 8)), dma((2, 8)), dma((2, 8, 4)), dma((2, 4, 8)),
            dma((2, 4)), dma((2, 4)), dma((2, 4)), dma((2, 4)),
        ],
        compiler_params=pltpu.CompilerParams(
            collective_id=0, has_side_effects=True, vmem_limit_bytes=60 * 1024 * 1024
        ),
        name="block",
    )(
        inputs,
        stale_kv,
        jnp.transpose(w_qkv, (1, 0, 2)),
        jnp.transpose(w_out),
        jnp.transpose(mod_table, (1, 0, 2)),
        step_ids,
        slab_order,
    )
    return out.reshape(2, TOK, FEAT)


def solution(mesh):
    in_specs = (
        P(None, "patch", "head"),
        P(None, "patch", "head"),
        P(None, None, "head"),
        P("head", "patch"),
        P(None, None, "head"),
        P(),
        P("patch"),
    )
    out_specs = P(None, "patch", "head")
    return jax.shard_map(body, mesh=mesh, in_specs=in_specs, out_specs=out_specs, check_vma=False)
```

```python
import functools
import math

import jax
import jax.numpy as jnp
from jax import lax
from jax.experimental import pallas as pl
from jax.experimental.pallas import tpu as pltpu
from jax.sharding import PartitionSpec as P

DH = 128
TOK = 32
FEAT = 384
HC = 256
WIDTH = 3072
OUTC = 48
NZ, NYH, NX, NYL = 8, 2, 4, 4
NB = NYH * NX
RELAY = frozenset([(0, 0), (0, 1), (0, 2), (0, 3), (0, 4), (0, 5), (0, 6), (0, 7), (1, 0), (1, 1), (1, 2), (1, 3), (1, 4), (1, 5), (1, 6), (1, 7)])
F32 = jnp.float32
BF16 = jnp.bfloat16
MESH = pl.DeviceIdType.MESH


def dot_nt(a, b):
    return lax.dot_general(a, b, (((1,), (1,)), ((), ())), preferred_element_type=F32)


def dot_nn(a, b):
    return jnp.dot(a, b, preferred_element_type=F32)


def kernel(
    x_ref, stale_ref, w_ref, wo_ref, mod_ref, ids_ref, order_ref, out_ref,
    ids_v, order_v, mod_v, w_v, xg, mg, a_v, kvs, kvf, kv1, qb, os_, orc, st, stc,
    wo, e0s, e0r, e1s, e1r, acc,
    in_sem, w_sem, xs_sem, xr_sem, ms_sem, mr_sem,
    ss_sem, sr_sem, fs_sem, fr_sem, qs_sem, qr_sem, os_sem, or_sem, ts_sem, tr_sem,
    wys_sem, wyr_sem, wzs_sem, wzr_sem, wxs_sem, wxr_sem,
    e0s_sem, e0r_sem, e1s_sem, e1r_sem,
):
    p = lax.axis_index("patch")
    h = lax.axis_index("head")
    z, b = p // NB, p % NB
    yh, x = b // NX, b % NX
    yl, c = h // 2, h % 2

    def z_peer(d):
        return (((z + d) % NZ) * NB + b, h)

    def x_peer(d):
        return (z * NB + yh * NX + (x + d) % NX, h)

    yh_peer = (z * NB + (1 - yh) * NX + x, h)
    sibling = (p, yl * 2 + 1 - c)

    def y_peer(d):
        return (p, ((yl + d) % NYL) * 2 + c)

    peers = [sibling, yh_peer]
    peers += [y_peer(d) for d in range(1, NYL)]
    peers += [x_peer(d) for d in range(1, NX)]
    peers += [z_peer(d) for d in range(1, NZ)]

    barrier = pltpu.get_barrier_semaphore()
    for peer in peers:
        pl.semaphore_signal(barrier, inc=1, device_id=peer, device_id_type=MESH)

    sent = []

    def send(src, dst, ssem, rsem, peer):
        copy = pltpu.make_async_remote_copy(
            src_ref=src, dst_ref=dst, send_sem=ssem, recv_sem=rsem, device_id=peer, device_id_type=MESH
        )
        copy.start()
        sent.append(copy)

    def arrived(dst, ssem, rsem, peer):
        pltpu.make_async_remote_copy(
            src_ref=dst, dst_ref=dst, send_sem=ssem, recv_sem=rsem, device_id=peer, device_id_type=MESH
        ).wait_recv()

    small = [
        pltpu.make_async_copy(ids_ref, ids_v, in_sem.at[0]),
        pltpu.make_async_copy(order_ref, order_v, in_sem.at[5]),
        pltpu.make_async_copy(mod_ref, mod_v, in_sem.at[1]),
        pltpu.make_async_copy(x_ref, xg.at[h], in_sem.at[2]),
        pltpu.make_async_copy(stale_ref, kvs.at[0], in_sem.at[3]),
        pltpu.make_async_copy(wo_ref, wo.at[z, yh, x], in_sem.at[4]),
    ]
    for load in small:
        load.start()
    loads = [pltpu.make_async_copy(w_ref.at[t], w_v.at[t], w_sem.at[t]) for t in range(3)]
    for t in (1, 2, 0):
        loads[t].start()
    for load in small[:3]:
        load.wait()

    table_row = lax.broadcasted_iota(jnp.int32, (4, FEAT), 0)
    gates = []
    for s in range(2):
        pick = table_row == ids_v[s]
        rows = [jnp.sum(jnp.where(pick, mod_v[k], 0.0), axis=0, keepdims=True) for k in range(3)]
        mg[h, s : s + 1] = rows[0]
        mg[h, 2 + s : 3 + s] = rows[1]
        gates.append(rows[2])
    token = lax.broadcasted_iota(jnp.int32, (TOK, DH), 0)
    lane = lax.broadcasted_iota(jnp.int32, (TOK, DH), 1)
    half = DH // 2
    exponent = jnp.where(lane < half, lane, lane - half).astype(F32) * (-math.log(10000.0) / half)
    angle = (order_v[0] * TOK + token).astype(F32) * jnp.exp(exponent)
    cos = jnp.cos(angle)
    sin = jnp.where(lane < half, -1.0, 1.0) * jnp.sin(angle)
    for load in small[3:]:
        load.wait()

    pl.semaphore_wait(barrier, len(peers))

    def wo_block(plane, dz, dx=0):
        return wo.at[(z + dz) % NZ, yh if plane == 0 else 1 - yh, (x + dx) % NX]

    relayed = set()

    def wo_along_x(plane, d):
        piece = wo_block(plane, d)
        for e in (1, 3) if (plane, d) in RELAY else (2, 1, 3):
            send(piece, piece, wxs_sem.at[plane, d, e], wxr_sem.at[plane, (NX - e) % NX, d], x_peer(e))

    def wo_relay(plane, d):
        e = 3 if plane == 0 else 1
        piece = wo_block(plane, d, e)
        arrived(piece, wxs_sem.at[plane, d, e], wxr_sem.at[plane, e, d], x_peer(e))
        send(piece, piece, wxs_sem.at[plane, d, 2], wxr_sem.at[plane, 2, d], x_peer(NX - e))
        relayed.add((plane, d, e))

    def wo_start(plane):
        piece = wo_block(plane, 0)
        for d in (1, 7, 2, 6, 3, 5, 4):
            send(piece, piece, wzs_sem.at[plane, d], wzr_sem.at[plane, NZ - d], z_peer(d))
        wo_along_x(plane, 0)

    def wo_forward(plane, d):
        arrived(wo_block(plane, d), wzs_sem.at[plane, d], wzr_sem.at[plane, d], z_peer(d))
        wo_along_x(plane, d)

    send(wo_block(0, 0), wo_block(0, 0), wys_sem, wyr_sem, yh_peer)
    for s in range(2):
        for d in (2, 1, 3):
            send(xg.at[h, s], xg.at[h, s], xs_sem.at[s, d], xr_sem.at[s, h], y_peer(d))
            if s == 0:
                send(mg.at[h], mg.at[h], ms_sem.at[d], mr_sem.at[h], y_peer(d))
        send(xg.at[h, s], xg.at[h, s], xs_sem.at[s, 0], xr_sem.at[s, h], sibling)
        if s == 0:
            send(mg.at[h], mg.at[h], ms_sem.at[0], mr_sem.at[h], sibling)
    wo_start(0)
    for d in range(1, NX):
        send(kvs.at[0], kvs.at[NX - d], ss_sem.at[d], sr_sem.at[NX - d], x_peer(d))
    send(kvs.at[0], kvs.at[NX], ss_sem.at[0], sr_sem.at[NX], yh_peer)

    def rows_forward(s):
        for d in (1, 3, 2):
            hs = ((yl + d) % NYL) * 2 + c
            arrived(xg.at[hs, s], xs_sem.at[s, d], xr_sem.at[s, hs], y_peer(d))
            send(xg.at[hs, s], xg.at[hs, s], xs_sem.at[s, NYL - 1 + d], xr_sem.at[s, hs], sibling)
            if s == 0:
                arrived(mg.at[hs], ms_sem.at[d], mr_sem.at[hs], y_peer(d))
                send(mg.at[hs], mg.at[hs], ms_sem.at[NYL - 1 + d], mr_sem.at[hs], sibling)

    def rows_done(s):
        for d in range(NYL):
            hs = ((yl + d) % NYL) * 2 + 1 - c
            arrived(xg.at[hs, s], xs_sem.at[s, 0], xr_sem.at[s, hs], sibling)
            if s == 0:
                arrived(mg.at[hs], ms_sem.at[0], mr_sem.at[hs], sibling)

    def normalize(s):
        sum1 = jnp.zeros((TOK, 128), F32)
        sum2 = jnp.zeros((TOK, 128), F32)
        for j in range(8):
            v = xg[j, s].astype(F32)
            for k in range(FEAT // 128):
                part = v[:, k * 128 : (k + 1) * 128]
                sum1 += part
                sum2 += part * part
        mean = jnp.sum(sum1, axis=1, keepdims=True) / WIDTH
        square = jnp.sum(sum2, axis=1, keepdims=True) / WIDTH
        inv = lax.rsqrt(square - mean * mean + 1e-06)
        for j in range(8):
            v = (xg[j, s].astype(F32) - mean) * inv
            v = v * (1.0 + mg[j, 2 + s : 3 + s]) + mg[j, s : s + 1]
            a_v[s, :, j * FEAT : (j + 1) * FEAT] = v.astype(BF16)

    def rot(u):
        heads = []
        for i in range(2):
            uh = u[:, i * DH : (i + 1) * DH]
            heads.append(uh * cos + pltpu.roll(uh, DH // 2, 1) * sin)
        return jnp.concatenate(heads, axis=1).astype(BF16)

    def project_in(s, own):
        if s == 0:
            loads[1].wait()
        own[0] = rot(dot_nn(a_v[s], w_v[1]))
        if s == 0:
            loads[2].wait()
        own[1] = dot_nn(a_v[s], w_v[2]).astype(BF16)

    def queries(s):
        if s == 0:
            loads[0].wait()
        qb[0, s] = rot(dot_nn(a_v[s], w_v[0]))
        for d in (4, 3, 5, 2, 6, 1, 7):
            send(qb.at[0, s], qb.at[NZ - d, s], qs_sem.at[s, d], qr_sem.at[s, NZ - d], z_peer(d))

    rows_forward(0)
    arrived(wo_block(1, 0), wys_sem, wyr_sem, yh_peer)
    wo_start(1)
    rows_done(0)
    normalize(0)
    project_in(0, kvf.at[0])
    send(kvf.at[0], kvf.at[NX], fs_sem.at[0], fr_sem.at[NX], yh_peer)
    for d in range(1, NX):
        send(kvf.at[0], kvf.at[NX - d], fs_sem.at[d], fr_sem.at[NX - d], x_peer(d))
    rows_forward(1)
    queries(0)

    arrived(kvs.at[NX], ss_sem.at[0], sr_sem.at[NX], yh_peer)
    for d in range(1, NX):
        send(kvs.at[NX], kvs.at[NX + NX - d], ss_sem.at[NX + d], sr_sem.at[NX + NX - d], x_peer(d))
    for d in (1, 7, 2, 6):
        wo_forward(0, d)

    rows_done(1)
    normalize(1)
    queries(1)
    project_in(1, kv1)
    for d in (0,):
        wo_relay(0, d)

    for d in (3, 5, 4):
        wo_forward(0, d)
    arrived(kvf.at[NX], fs_sem.at[0], fr_sem.at[NX], yh_peer)
    for d in range(1, NX):
        send(kvf.at[NX], kvf.at[NX + NX - d], fs_sem.at[NX + d], fr_sem.at[NX + NX - d], x_peer(d))
    for d in (1, 7, 2, 6):
        wo_forward(1, d)
    for d in (1, 7, 2, 6,):
        wo_relay(0, d)
    for d in (0,):
        wo_relay(1, d)

    inv_root = 1.0 / math.sqrt(DH)
    ones = jnp.ones((NB * TOK, DH), BF16)
    diagonal = lax.broadcasted_iota(jnp.int32, (128, 128), 0) == lax.broadcasted_iota(jnp.int32, (128, 128), 1)

    def attend(s, held, own):
        for i in range(2):
            cols = slice(i * DH, (i + 1) * DH)
            keys = held[:, 0, :, cols].reshape(NB * TOK, DH)
            vals = held[:, 1, :, cols].reshape(NB * TOK, DH)
            own_keys = jnp.concatenate([own[0, :, cols], keys[TOK:]], axis=0)
            own_vals = jnp.concatenate([own[1, :, cols], vals[TOK:]], axis=0)
            q = qb[:, s, :, cols].reshape(NZ * TOK, DH)
            scores = jnp.concatenate([dot_nt(q[:TOK], own_keys), dot_nt(q[TOK:], keys)], axis=0) * inv_root
            top = jnp.max(scores, axis=1, keepdims=True)
            weights = jnp.exp(scores - top).astype(BF16)
            mixed = jnp.concatenate(
                [
                    dot_nn(weights[:TOK], jnp.concatenate([own_vals, ones], axis=1)),
                    dot_nn(weights[TOK:], jnp.concatenate([vals, ones], axis=1)),
                ],
                axis=0,
            )
            total = mixed[:, DH:]
            os_[s, :, :, cols] = (mixed[:, :DH] / total).astype(BF16).reshape(NZ, TOK, DH)
            lse = top + jnp.log(total)
            for k in range(NZ * TOK // 128):
                part = lse[k * 128 : (k + 1) * 128]
                row = jnp.sum(jnp.where(diagonal, part, 0.0), axis=0, keepdims=True)
                st[s, i : i + 1, k * 128 : (k + 1) * 128] = row
        for d in (4, 3, 5, 2, 6, 1, 7):
            send(os_.at[s, d], orc.at[s, NZ - d], os_sem.at[s, d], or_sem.at[s, NZ - d], z_peer(d))
            send(st.at[s], stc.at[s, NZ - d], ts_sem.at[s, d], tr_sem.at[s, NZ - d], z_peer(d))

    for d in range(1, NX):
        arrived(kvs.at[d], ss_sem.at[d], sr_sem.at[d], x_peer(d))
        arrived(kvs.at[NX + d], ss_sem.at[NX + d], sr_sem.at[NX + d], x_peer(d))
    for d in range(1, NZ):
        arrived(qb.at[d, 0], qs_sem.at[0, d], qr_sem.at[0, d], z_peer(d))
    attend(0, kvs, kvf.at[0])
    for d in (3, 5, 4):
        wo_forward(1, d)
    for d in (3, 5, 4,):
        wo_relay(0, d)


    for d in range(1, NX):
        arrived(kvf.at[d], fs_sem.at[d], fr_sem.at[d], x_peer(d))
        arrived(kvf.at[NX + d], fs_sem.at[NX + d], fr_sem.at[NX + d], x_peer(d))
    for d in range(1, NZ):
        arrived(qb.at[d, 1], qs_sem.at[1, d], qr_sem.at[1, d], z_peer(d))
    early = list(sent)
    attend(1, kvf, kv1)
    for d in (1, 7, 2, 6, 3, 5, 4,):
        wo_relay(1, d)

    row_id = lax.broadcasted_iota(jnp.int32, (TOK, 128), 0)
    lane_id = lax.broadcasted_iota(jnp.int32, (TOK, 128), 1)

    def merge(s):
        for d in range(1, NZ):
            arrived(orc.at[s, d], os_sem.at[s, d], or_sem.at[s, d], z_peer(d))
            arrived(stc.at[s, d], ts_sem.at[s, d], tr_sem.at[s, d], z_peer(d))
        heads = []
        for i in range(2):
            lse = []
            for d in range(NZ):
                held = st if d == 0 else stc.at[:, d]
                at = (NZ - d) % NZ * TOK
                row = held[s, i : i + 1, at // 128 * 128 : at // 128 * 128 + 128]
                lse.append(jnp.sum(jnp.where(lane_id == row_id + at % 128, row, 0.0), axis=1, keepdims=True))
            top = functools.reduce(jnp.maximum, lse)
            mixed = jnp.zeros((TOK, DH), F32)
            total = jnp.zeros((TOK, 1), F32)
            for d in range(NZ):
                weight = jnp.exp(lse[d] - top)
                total += weight
                part = (os_ if d == 0 else orc)[s, d, :, i * DH : (i + 1) * DH]
                mixed += weight * part.astype(F32)
            heads.append((mixed / total).astype(BF16))
        return jnp.concatenate(heads, axis=1)

    def block(o, j, core):
        return dot_nt(o, wo[((yl + j) % NYL) * 2 + core].reshape(FEAT, HC))

    def wo_collect(offsets):
        for e in range(1, NX):
            for d in offsets:
                for plane in range(NYH):
                    if (plane, d, e) in relayed:
                        continue
                    arrived(wo_block(plane, d, e), wxs_sem.at[plane, d, e], wxr_sem.at[plane, e, d], x_peer(e))

    def project(s):
        o = merge(s)
        if s == 0:
            wo_collect((3, 5, 4))
        for j in (2, 1, 3, 0):
            e0s[s, j] = block(o, j, 1 - c).astype(BF16)
            send(e0s.at[s, j], e0r.at[s, j], e0s_sem.at[s, j], e0r_sem.at[s, j], sibling)
        for j in (2, 1, 3, 0):
            mine = block(o, j, c)
            arrived(e0r.at[s, j], e0s_sem.at[s, j], e0r_sem.at[s, j], sibling)
            mine = mine + e0r[s, j].astype(F32)
            if j:
                e1s[s, j] = mine.astype(BF16)
                send(e1s.at[s, j], e1r.at[s, NYL - j], e1s_sem.at[s, j], e1r_sem.at[s, NYL - j], y_peer(j))
            else:
                acc[s] = mine

    for copy in early:
        copy.wait_send()
    wo_collect((0, 1, 7, 2, 6))
    project(0)
    project(1)
    for s in range(2):
        total = acc[s]
        for j in range(1, NYL):
            arrived(e1r.at[s, j], e1s_sem.at[s, j], e1r_sem.at[s, j], y_peer(j))
            total = total + e1r[s, j].astype(F32)
        out_ref[s * TOK : (s + 1) * TOK] = (gates[s] * total).astype(BF16)

    for copy in sent[len(early) :]:
        copy.wait_send()


def body(inputs, stale_kv, w_qkv, w_out, mod_table, step_ids, slab_order):
    vmem = pl.BlockSpec(memory_space=pltpu.VMEM)
    dma = pltpu.SemaphoreType.DMA
    out = pl.pallas_call(
        kernel,
        out_shape=jax.ShapeDtypeStruct((2 * TOK, FEAT), BF16),
        in_specs=[pl.BlockSpec(memory_space=pltpu.HBM)] * 7,
        out_specs=vmem,
        scratch_shapes=[
            pltpu.SMEM((2,), jnp.int32),
            pltpu.SMEM((1,), jnp.int32),
            pltpu.VMEM((3, 4, FEAT), F32),
            pltpu.VMEM((3, WIDTH, HC), BF16),
            pltpu.VMEM((8, 2, TOK, FEAT), BF16),
            pltpu.VMEM((8, 4, FEAT), F32),
            pltpu.VMEM((2, TOK, WIDTH), BF16),
            pltpu.VMEM((NB, 2, TOK, HC), BF16),
            pltpu.VMEM((NB, 2, TOK, HC), BF16),
            pltpu.VMEM((2, TOK, HC), BF16),
            pltpu.VMEM((NZ, 2, TOK, HC), BF16),
            pltpu.VMEM((2, NZ, TOK, HC), BF16),
            pltpu.VMEM((2, NZ, TOK, HC), BF16),
            pltpu.VMEM((2, 2, NZ * TOK), F32),
            pltpu.VMEM((2, NZ, 2, NZ * TOK), F32),
            pltpu.VMEM((NZ, NYH, NX, OUTC, HC), BF16),
            pltpu.VMEM((2, NYL, TOK, FEAT), BF16),
            pltpu.VMEM((2, NYL, TOK, FEAT), BF16),
            pltpu.VMEM((2, NYL, TOK, FEAT), BF16),
            pltpu.VMEM((2, NYL, TOK, FEAT), BF16),
            pltpu.VMEM((2, TOK, FEAT), F32),
            dma((6,)), dma((3,)),
            dma((2, 7)), dma((2, 8)), dma((7,)), dma((8,)),
            dma((8,)), dma((8,)), dma((8,)), dma((8,)),
            dma((2, 8)), dma((2, 8)), dma((2, 8)), dma((2, 8)), dma((2, 8)), dma((2, 8)),
            dma, dma, dma((2, 8)), dma((2, 8)), dma((2, 8, 4)), dma((2, 4, 8)),
            dma((2, 4)), dma((2, 4)), dma((2, 4)), dma((2, 4)),
        ],
        compiler_params=pltpu.CompilerParams(
            collective_id=0, has_side_effects=True, vmem_limit_bytes=60 * 1024 * 1024
        ),
        name="block",
    )(
        inputs,
        stale_kv,
        jnp.transpose(w_qkv, (1, 0, 2)),
        jnp.transpose(w_out),
        jnp.transpose(mod_table, (1, 0, 2)),
        step_ids,
        slab_order,
    )
    return out.reshape(2, TOK, FEAT)


def solution(mesh):
    in_specs = (
        P(None, "patch", "head"),
        P(None, "patch", "head"),
        P(None, None, "head"),
        P("head", "patch"),
        P(None, None, "head"),
        P(),
        P("patch"),
    )
    out_specs = P(None, "patch", "head")
    return jax.shard_map(body, mesh=mesh, in_specs=in_specs, out_specs=out_specs, check_vma=False)
```
